32 devices in a mesh: dp: 2 (over x), expert: 16 (over z, y, core).
Axes of the slice: x: 2, y: 2, z: 4, core: 2. Of those that a mesh axis runs over, the one named last changes fastest.
Arguments:
- tokens: bfloat16 [256, 4096], P(('dp', 'expert')), may hold values from -6 to 6
- cotangent: bfloat16 [256, 4096], P(('dp', 'expert')), may hold values from -6 to 6
- gates: float32 [256, 8], P(('dp', 'expert')), may hold values from 0.1 to 0.5
- expert_ids: int32 [256, 8], P(('dp', 'expert')), may hold values from 0 to 15, all different within a row; in each aligned block of 8 rows (0 to 7, 8 to 15, ...) at most 8 rows name the same one
- swap_flag: int32 [16], replicated, may hold values from 0 to 1, as said below
- w_in: bfloat16 [16, 2, 768, 4096], P('expert', None, 'dp'), may hold values from -0.09375 to 0.09375
- w_down: bfloat16 [16, 768, 4096], P('expert', 'dp'), may hold values from -0.21875 to 0.21875
Outputs:
- mixed: bfloat16 [256, 4096], P(('dp', 'expert'))
- grad_tokens: bfloat16 [256, 4096], P(('dp', 'expert'))
- grad_in: bfloat16 [16, 2, 768, 4096], P('expert', None, 'dp')
- grad_down: bfloat16 [16, 768, 4096], P('expert', 'dp')
The draws below stay inside these ranges and needn't reach their ends.
Inputs may be any that keep to these rules, and one draw needn't show every extreme that they name: `expert_ids`: each row names 8 different experts; in the rows of one device no expert is named more than 8 times. swap_flag[e] equals swap_flag[(e + 8) mod 16]; both values occur.
All inputs are finite; a program needn't handle non-finite values.
Results may differ from the reference program's by a relative error of at most 0.014.
Values may be sent and summed in bfloat16 or wider, within the bound.
No kernel may reach another device: no remote copies, remote signals or barrier semaphores. Data moves between devices by JAX's collectives and lax.ppermute only.
A program may use at most 128 MiB of HBM per device.

```python
import math
import jax
import jax.numpy as jnp
import numpy as np
from jax import lax

D = 4096
TOP = 8
FF = 768
TOK_DEV = 8
EXPERTS = 16
CAP = 8
TOKENS = 256
N_DP = 2


def draw_swap_flag(key, part):
    half_count = EXPERTS // 2
    random_bits = jax.random.randint(key, (half_count,), 0, 2)
    fixed_bits = random_bits.at[0].set(1).at[1].set(0)
    shuffled = jax.random.permutation(jax.random.fold_in(key, 7), fixed_bits)
    return jnp.concatenate([shuffled, shuffled]).astype(jnp.int32)


def levels(own_key, shape, split, smallest, top_value):
    factor_of, own = 1.0, jax.random.fold_in(own_key, 6)
    for dim, shards_of in split:
        draws = jnp.exp(jax.random.uniform(jax.random.fold_in(own, dim), (shards_of,), jnp.float32, smallest / len(split), top_value / len(split)))
        factor_of = factor_of * jnp.repeat(draws, shape[dim] // shards_of).reshape([-1 if axis == dim else 1 for axis in range(len(shape))])
    return factor_of


def routed_block(key, own, number, rows, number_of, top, limit, skew):
    sequence = jax.random.permutation(key, number_of)
    packed, ordinary = shares(number_of, rows * top, limit, skew, True), shares(number_of, rows * top, limit, skew, False)
    places = jnp.arange(number_of)

    def named(tallies, rotation):
        used = int((tallies > 0).sum())
        fixed = max(1, used // 4)
        moved = fixed + (places - fixed + rotation * (used - fixed)) % max(1, number_of - fixed)
        return jnp.zeros((number_of,), jnp.int32).at[sequence[jnp.where(places < fixed, places, moved)]].set(jnp.asarray(tallies, jnp.int32))

    tallies = jnp.where(number % 4 == 0, named(packed, number // 4), named(ordinary, number - number // 4 - 1))
    mixed = jax.random.permutation(jax.random.fold_in(own, 3), number_of)
    source_of, receiver = mixed[0:number_of // 2 * 2:2], mixed[1:number_of // 2 * 2:2]
    room = jnp.minimum(tallies[source_of] - 1, limit - tallies[receiver]) // 2
    room = jnp.where((source_of == sequence[0]) | (receiver == sequence[0]) | (tallies[receiver] == 0), 0, jnp.maximum(room, 0))
    moved = jax.random.randint(jax.random.fold_in(own, 4), (number_of // 2,), 0, 1 << 20) % (room + 1)
    tallies = tallies.at[source_of].add(-moved).at[receiver].add(moved)
    items = jnp.searchsorted(jnp.cumsum(tallies), jnp.arange(rows * top), side="right").astype(jnp.int32)
    listing = items.reshape(top, rows).T
    listing = listing[jax.random.permutation(jax.random.fold_in(own, 1), rows)]
    rotation = jax.random.randint(jax.random.fold_in(own, 2), (rows, 1), 0, top)
    return jnp.take_along_axis(listing, (jnp.arange(top)[None, :] + rotation) % top, axis=1)


def shares(number_of, total, most, skew, full):
    portions = [(1 << 20) // math.isqrt(rank ** skew) + 1 for rank in range(1, number_of + 1)]
    largest = most if full else min(most, max(-(-total // number_of), total * portions[0] // sum(portions)))
    least = 1 if total - largest >= number_of - 1 else 0
    given, rest = [largest] + [least] * (number_of - 1), total - largest - least * (number_of - 1)
    while rest > 0:
        candidates = [i for i in range(1, number_of) if given[i] < largest] or [i for i in range(1, number_of) if given[i] < most]
        mass, budget = sum([portions[i] for i in candidates]), rest
        for i in candidates:
            addition = min(most - given[i], max(1, budget * portions[i] // mass), rest)
            given[i] = given[i] + addition
            rest = rest - addition
    return np.array(given)


def noise(rng, shape, width, most, pieces=(), held_as=jnp.bfloat16):
    drawn = width * jax.random.normal(rng, shape, jnp.float32)
    if pieces:
        drawn = drawn * levels(rng, shape, pieces, -0.22, 0.18)
    return jnp.clip(drawn, -most, most).astype(held_as)


def setup_inputs(seed: int = 0) -> dict:
    keys = jax.random.split(jax.random.key(seed), 8)
    tokens = noise(keys[0], (TOKENS, D), 1.0, 6.0, ((0, 32),))
    cotangent = noise(keys[1], (TOKENS, D), 1.0, 6.0, ((0, 32),))
    gates = jnp.clip(0.1 + 0.4 * jax.random.uniform(keys[2], (TOKENS, TOP), jnp.float32) ** levels(keys[2], (TOKENS, TOP), ((0, 32),), -0.2, 0.2), 0.1, 0.5)
    expert_ids_keys = jax.random.split(jax.random.fold_in(keys[3], 1), TOKENS // TOK_DEV)
    expert_ids_turns = jax.random.permutation(jax.random.fold_in(keys[3], 3), TOKENS // TOK_DEV)
    expert_ids = jax.vmap(lambda own, number: routed_block(jax.random.fold_in(keys[3], 2), own, number, TOK_DEV, EXPERTS, TOP, CAP, 2))(expert_ids_keys, expert_ids_turns).reshape((TOKENS, TOP))
    swap_flag = draw_swap_flag(jax.random.fold_in(keys[7], 71), 0)
    w_in = noise(keys[5], (EXPERTS, 2, FF, D), D ** -0.5, 0.09375, ((0, 16), (2, 2)))
    w_down = noise(keys[6], (EXPERTS, FF, D), FF ** -0.5, 0.21875, ((0, 16), (1, 2)))
    return {"tokens": tokens, "cotangent": cotangent, "gates": gates, "expert_ids": expert_ids, "swap_flag": swap_flag, "w_in": w_in, "w_down": w_down}


def reference(tokens, cotangent, gates, expert_ids, swap_flag, w_in, w_down):
    blocks = TOKENS // TOK_DEV
    half_axis = EXPERTS // 2
    unit_count = FF // N_DP
    row_total = blocks * CAP
    flat_ids = expert_ids.reshape(blocks, TOK_DEV * TOP)
    targets = (flat_ids + half_axis * swap_flag[flat_ids]) % EXPERTS
    onehot = (targets[:, :, None] == jnp.arange(EXPERTS, dtype=jnp.int32)[None, None, :]).astype(jnp.int32)
    earlier = jnp.cumsum(onehot, axis=1) - onehot
    position = jnp.sum(earlier * onehot, axis=2)
    row_slot = jnp.arange(blocks, dtype=jnp.int32)[:, None] * CAP + position
    entry_ids = jnp.arange(TOKENS * TOP, dtype=jnp.int32).reshape(blocks, TOK_DEV * TOP)
    row_table = jnp.full((EXPERTS, row_total), -1, jnp.int32)
    row_table = row_table.at[targets.reshape(-1), row_slot.reshape(-1)].set(entry_ids.reshape(-1))
    scaled = (gates[:, :, None] * cotangent.astype(jnp.float32)[:, None, :]).astype(jnp.bfloat16)
    scaled = scaled.reshape(TOKENS * TOP, D)
    slot_ids = jnp.arange(EXPERTS, dtype=jnp.int32)
    slot_owner = (slot_ids + half_axis * swap_flag) % EXPERTS

    def one_slot(slot_args):
        slot_index, expert = slot_args
        is_filled = (slot_index >= 0)[:, None]
        safe_index = jnp.maximum(slot_index, 0)
        rows_x = jnp.where(is_filled, tokens[safe_index // TOP], jnp.zeros((), jnp.bfloat16))
        rows_do = jnp.where(is_filled, scaled[safe_index], jnp.zeros((), jnp.bfloat16))
        weight_in = lax.dynamic_index_in_dim(w_in, expert, 0, keepdims=False)
        weight_down = lax.dynamic_index_in_dim(w_down, expert, 0, keepdims=False)
        grouped_in = weight_in.reshape(2, N_DP, unit_count, D).transpose(1, 0, 2, 3)
        grouped_in = grouped_in.reshape(N_DP, 2 * unit_count, D).astype(jnp.float32)
        grouped_down = weight_down.reshape(N_DP, unit_count, D).astype(jnp.float32)
        rows_xf = rows_x.astype(jnp.float32)
        rows_dof = rows_do.astype(jnp.float32)
        hidden = jnp.einsum('rd,qfd->qrf', rows_xf, grouped_in)
        gate_part = hidden[:, :, :unit_count]
        up_part = hidden[:, :, unit_count:]
        sigmoid_gate = jax.nn.sigmoid(gate_part)
        silu_gate = gate_part * sigmoid_gate
        activation = (silu_gate * up_part).astype(jnp.bfloat16)
        partial_value = jnp.einsum('qrf,qfd->qrd', activation.astype(jnp.float32), grouped_down).astype(jnp.bfloat16)
        expert_out = jnp.sum(partial_value.astype(jnp.float32), axis=0).astype(jnp.bfloat16)
        grad_act = jnp.einsum('rd,qfd->qrf', rows_dof, grouped_down)
        grad_up = (grad_act * silu_gate).astype(jnp.bfloat16)
        grad_gate = (grad_act * up_part * sigmoid_gate * (1.0 + gate_part * (1.0 - sigmoid_gate))).astype(jnp.bfloat16)
        grad_hidden = jnp.concatenate([grad_gate, grad_up], axis=2).astype(jnp.float32)
        grad_down_q = jnp.einsum('qrf,rd->qfd', activation.astype(jnp.float32), rows_dof).astype(jnp.bfloat16)
        grad_in_q = jnp.einsum('qrf,rd->qfd', grad_hidden, rows_xf).astype(jnp.bfloat16)
        grad_in_e = grad_in_q.reshape(N_DP, 2, unit_count, D).transpose(1, 0, 2, 3).reshape(2, FF, D)
        back_part = jnp.einsum('qrf,qfd->qrd', grad_hidden, grouped_in).astype(jnp.bfloat16)
        grad_rows = jnp.sum(back_part.astype(jnp.float32), axis=0).astype(jnp.bfloat16)
        return expert_out, grad_rows, grad_in_e, grad_down_q.reshape(FF, D)

    out_all, back_all, grad_in, grad_down = lax.map(one_slot, (row_table, slot_owner))
    picked_out = out_all[targets, row_slot].reshape(TOKENS, TOP, D)
    picked_back = back_all[targets, row_slot].reshape(TOKENS, TOP, D)
    mixed = jnp.sum(gates[:, :, None] * picked_out.astype(jnp.float32), axis=1).astype(jnp.bfloat16)
    grad_tokens = jnp.sum(picked_back.astype(jnp.float32), axis=1).astype(jnp.bfloat16)
    return (mixed, grad_tokens, grad_in, grad_down)
```

```python
import jax
import jax.numpy as jnp
from jax import lax
from jax.sharding import PartitionSpec as P

ALL = ("dp", "expert")
F32, BF16 = jnp.float32, jnp.bfloat16


def split_three(x):
    high = x.astype(BF16)
    rest = x - high.astype(F32)
    middle = rest.astype(BF16)
    low = (rest - middle.astype(F32)).astype(BF16)
    return high, middle, low


def nt(a, b):
    return lax.dot_general(a, b, (((1,), (1,)), ((), ())), preferred_element_type=F32)


def tn(a, b):
    return lax.dot_general(a, b, (((0,), (0,)), ((), ())), preferred_element_type=F32)


def on_device(tokens, cotangent, gates, expert_ids, swap_flag, w_in, w_down):
    experts = lax.axis_size("expert")
    half_axis = experts // 2
    dim = tokens.shape[1]
    me = lax.axis_index("expert")
    slots = jnp.arange(experts, dtype=jnp.int32)
    flag = jnp.sum(jnp.where(slots == me, swap_flag, 0))
    held = jnp.where(flag > 0, (me + half_axis) % experts, me)
    own_in = w_in.reshape(-1, dim)
    own_down = w_down.reshape(-1, dim)
    units = own_down.shape[0]

    dense = jnp.sum(
        jnp.where(expert_ids[:, :, None] == slots, gates[:, :, None], 0.0), axis=1
    )
    parts = jnp.concatenate(split_three(dense), axis=1)
    width = parts.shape[1]
    parts = jnp.pad(parts, ((0, 0), (0, -width % 128)))
    packed = jnp.concatenate([tokens, cotangent, parts], axis=1)
    rows = lax.all_gather(packed, ALL, axis=0, tiled=True)
    rows_x = rows[:, :dim]
    cot = rows[:, dim : 2 * dim].astype(F32)
    pieces = rows[:, 2 * dim : 2 * dim + width].astype(F32)

    def gate_of(expert):
        match = (jnp.arange(width) % experts) == expert
        chosen = jnp.where(match, pieces, 0.0).reshape(-1, 3, experts)
        a, b, c = (jnp.sum(chosen[:, i], axis=1) for i in range(3))
        return ((c + b) + a)[:, None]

    gate_own = gate_of(me)
    rows_do = (gate_own * cot).astype(BF16)
    rows_do_held = (gate_of(held) * cot).astype(BF16)

    hidden = nt(rows_x, own_in)
    g, u = hidden[:, :units], hidden[:, units:]
    sig = jax.nn.sigmoid(g)
    silu = g * sig
    act = (silu * u).astype(BF16)
    grad_act = nt(rows_do, own_down)
    grad_u = (grad_act * silu).astype(BF16)
    grad_g = (grad_act * u * sig * (1.0 + g * (1.0 - sig))).astype(BF16)
    grad_hidden = jnp.concatenate([grad_g, grad_u], axis=1)

    factors = jnp.concatenate([act, grad_hidden], axis=1)
    route = [(i, (i + half_axis) % experts) for i in range(experts)]
    far = lax.ppermute(factors, "expert", route)

    part = jnp.dot(act, own_down, preferred_element_type=F32).astype(BF16)
    mine = (gate_own * part.astype(F32)).astype(BF16)
    mixed = lax.psum_scatter(mine, ALL, scatter_dimension=0, tiled=True)
    back = jnp.dot(grad_hidden, own_in, preferred_element_type=F32).astype(BF16)
    grad_tokens = lax.psum_scatter(back, ALL, scatter_dimension=0, tiled=True)

    used = jnp.where(flag > 0, far, factors)
    new_down = tn(used[:, :units], rows_do_held).astype(BF16)
    new_in = tn(used[:, units:], rows_x).astype(BF16)
    return (mixed, grad_tokens, new_in.reshape(w_in.shape), new_down.reshape(w_down.shape))


def solution(mesh):
    rows = P(ALL, None)
    w_in, w_down = P("expert", None, "dp", None), P("expert", "dp", None)
    return jax.shard_map(
        on_device,
        mesh=mesh,
        in_specs=(rows, rows, rows, rows, P(), w_in, w_down),
        out_specs=(rows, rows, w_in, w_down),
        check_vma=False,
    )
```

```python
import jax
import jax.numpy as jnp
from jax import lax
from jax.sharding import PartitionSpec as P

F32, BF16 = jnp.float32, jnp.bfloat16


def split_three(x):
    high = x.astype(BF16)
    rest = x - high.astype(F32)
    middle = rest.astype(BF16)
    low = (rest - middle.astype(F32)).astype(BF16)
    return high, middle, low


def nt(a, b):
    return lax.dot_general(a, b, (((1,), (1,)), ((), ())), preferred_element_type=F32)


def tn(a, b):
    return lax.dot_general(a, b, (((0,), (0,)), ((), ())), preferred_element_type=F32)


def masks(axis):
    size, out = lax.axis_size(axis), []
    while size > 1:
        size //= 2
        out.append((axis, size))
    return out


def partner(block, bit):
    axis, mask = bit
    return lax.ppermute(block, axis, [(i, i ^ mask) for i in range(lax.axis_size(axis))])


def inner_rows(bit, done, order, unit):
    for other in done:
        if order.index(other) > order.index(bit):
            unit *= 2
    return unit


def ordered(pair, bit, fixed):
    if bit != fixed:
        return pair
    axis, mask = bit
    turned = (lax.axis_index(axis) & mask) > 0
    return [jnp.where(turned, pair[1 - i], pair[i]) for i in (0, 1)]


def gather(block, route, order, fixed):
    unit, done = block.shape[0], []
    for bit in route:
        inner = inner_rows(bit, done, order, unit)
        pair = ordered([block, partner(block, bit)], bit, fixed)
        pair = [part.reshape(-1, inner, part.shape[1]) for part in pair]
        block = jnp.concatenate(pair, axis=1).reshape(-1, block.shape[1])
        done.append(bit)
    return block


def halves(block, inner):
    split = block.reshape(-1, 2, inner, block.shape[1])
    return [split[:, i].reshape(-1, block.shape[1]) for i in (0, 1)]


def scatter_sum(block, route, order, fixed, unit):
    left = list(route)
    keep = block
    for bit in route:
        left.remove(bit)
        kept, sent = ordered(halves(keep, inner_rows(bit, left, order, unit)), bit, fixed)
        got = partner(sent, bit)
        keep = (kept.astype(F32) + got.astype(F32)).astype(BF16)
    return keep


def on_device(tokens, cotangent, gates, expert_ids, swap_flag, w_in, w_down):
    experts = lax.axis_size("expert")
    half_axis = experts // 2
    tok_dev, dim = tokens.shape
    me = lax.axis_index("expert")
    slots = jnp.arange(experts, dtype=jnp.int32)
    flag = jnp.sum(jnp.where(slots == me, swap_flag, 0))
    held = jnp.where(flag > 0, (me + half_axis) % experts, me)
    own_in = w_in.reshape(-1, dim)
    own_down = w_down.reshape(-1, dim)
    units = own_down.shape[0]

    across, within = masks("dp"), masks("expert")
    core, near, far = within[-1:], within[-2:-1], within[:-2]
    first = far + near + across + core
    second = far + across + near + core
    order = first[::-1]

    dense = jnp.sum(
        jnp.where(expert_ids[:, :, None] == slots, gates[:, :, None], 0.0), axis=1
    )
    parts = jnp.concatenate(split_three(dense), axis=1)
    width = parts.shape[1]
    parts = jnp.pad(parts, ((0, 0), (0, -width % 128)))
    rows_x = gather(tokens, first, order, far[0])
    packed = gather(jnp.concatenate([cotangent, parts], axis=1), second, order, far[0])
    cot = packed[:, :dim].astype(F32)
    pieces = packed[:, dim : dim + width].astype(F32)

    def gate_of(expert):
        match = (jnp.arange(width) % experts) == expert
        chosen = jnp.where(match, pieces, 0.0).reshape(-1, 3, experts)
        a, b, c = (jnp.sum(chosen[:, i], axis=1) for i in range(3))
        return ((c + b) + a)[:, None]

    gate_own = gate_of(me)
    rows_do = (gate_own * cot).astype(BF16)
    rows_do_held = (gate_of(held) * cot).astype(BF16)

    hidden = nt(rows_x, own_in)
    g, u = hidden[:, :units], hidden[:, units:]
    sig = jax.nn.sigmoid(g)
    silu = g * sig
    act = (silu * u).astype(BF16)
    grad_act = nt(rows_do, own_down)
    grad_u = (grad_act * silu).astype(BF16)
    grad_g = (grad_act * u * sig * (1.0 + g * (1.0 - sig))).astype(BF16)
    grad_hidden = jnp.concatenate([grad_g, grad_u], axis=1)

    factors = jnp.concatenate([act, grad_hidden], axis=1)
    away = partner(factors, ("expert", half_axis))

    part = jnp.dot(act, own_down, preferred_element_type=F32).astype(BF16)
    mine = (gate_own * part.astype(F32)).astype(BF16)
    mixed = scatter_sum(mine, first[::-1], order, far[0], tok_dev)
    back = jnp.dot(grad_hidden, own_in, preferred_element_type=F32).astype(BF16)
    grad_tokens = scatter_sum(back, second[::-1], order, far[0], tok_dev)

    used = jnp.where(flag > 0, away, factors)
    new_down = tn(used[:, :units], rows_do_held).astype(BF16)
    new_in = tn(used[:, units:], rows_x).astype(BF16)
    return (mixed, grad_tokens, new_in.reshape(w_in.shape), new_down.reshape(w_down.shape))


def solution(mesh):
    rows = P(("dp", "expert"), None)
    w_in, w_down = P("expert", None, "dp", None), P("expert", "dp", None)
    return jax.shard_map(
        on_device,
        mesh=mesh,
        in_specs=(rows, rows, rows, rows, P(), w_in, w_down),
        out_specs=(rows, rows, w_in, w_down),
        check_vma=False,
    )
```

```python
import functools

import jax
import jax.numpy as jnp
from jax import lax
from jax.experimental import pallas as pl
from jax.experimental.pallas import tpu as pltpu
from jax.sharding import PartitionSpec as P

F32, BF16 = jnp.float32, jnp.bfloat16
ANY = pl.BlockSpec(memory_space=pl.ANY)
SMEM = pl.BlockSpec(memory_space=pltpu.SMEM)
VMEM = pl.BlockSpec(memory_space=pltpu.VMEM)
CHUNKS = 4
ROW_BLOCK = 256


def split_three(x):
    high = x.astype(BF16)
    rest = x - high.astype(F32)
    middle = rest.astype(BF16)
    low = (rest - middle.astype(F32)).astype(BF16)
    return high, middle, low


def nt(a, b):
    return lax.dot_general(a, b, (((1,), (1,)), ((), ())), preferred_element_type=F32)


def nn(a, b):
    return jnp.dot(a, b, preferred_element_type=F32)


def each_rows(total, body):
    if total <= ROW_BLOCK:
        body(pl.ds(0, total))
    else:

        @pl.loop(0, total // ROW_BLOCK)
        def _(i):
            body(pl.ds(pl.multiple_of(i * ROW_BLOCK, ROW_BLOCK), ROW_BLOCK))


def columns(dim):
    step = dim // CHUNKS
    return [pl.ds(c * step, step) for c in range(CHUNKS)]


def started(sems, base, pairs):
    copies = [
        pltpu.make_async_copy(source, target, sems.at[base + i])
        for i, (source, target) in enumerate(pairs)
    ]
    for copy in copies:
        copy.start()
    return copies


def wait(copies):
    for copy in copies:
        copy.wait()


def two_halves(first, second, buffer, cols):
    half = first.shape[0]
    return [
        (first.at[:, cols], buffer.at[pl.ds(0, half), cols]),
        (second.at[:, cols], buffer.at[pl.ds(half, half), cols]),
    ]


def gate_column(parts, expert, experts):
    lane = lax.broadcasted_iota(jnp.int32, parts.shape, 1)
    values = parts.astype(F32)
    high, middle, low = (
        jnp.sum(jnp.where(lane == expert + i * experts, values, 0.0), axis=1, keepdims=True)
        for i in range(3)
    )
    return (low + middle) + high


def fill_gates(buffer, gate, dim, expert, experts):
    width = buffer.shape[1] - dim

    def body(rows):
        column = gate_column(buffer[rows, pl.ds(dim, width)], expert, experts)
        gate[rows, :] = jnp.broadcast_to(column, (column.shape[0], gate.shape[1]))

    each_rows(buffer.shape[0], body)


def clear_pad(buffer, units, padded):
    if padded > units:
        for start in range(0, buffer.shape[0], padded):
            buffer[pl.ds(start + units, padded - units), :] = jnp.zeros(
                (padded - units, buffer.shape[1]), buffer.dtype
            )


def in_pairs(w_in, buffer, units, padded, cols):
    return [
        (w_in.at[i, :, cols], buffer.at[pl.ds(i * padded, units), cols]) for i in (0, 1)
    ]


def forward_kernel(
    experts, units, place, xa, xb, w_in, w_down, act, silu, slope, keep, send,
    x, win, wdown, hidden, gate, out, sems,
):
    dim = w_down.shape[1]
    rows_all, half, padded = x.shape[0], x.shape[0] // 2, act.shape[1]
    width = x.shape[1] - dim
    parts = started(sems, 0, two_halves(xa, xb, x, pl.ds(dim, width)))
    base, loads = 2, []
    for cols in columns(dim):
        pairs = two_halves(xa, xb, x, cols) + in_pairs(w_in, win, units, padded, cols)
        loads.append(started(sems, base, pairs))
        base += len(pairs)
    down = []
    for cols in columns(dim):
        down.append(started(sems, base, [(w_down.at[:, cols], wdown.at[pl.ds(0, units), cols])]))
        base += 1
    clear_pad(win, units, padded)
    clear_pad(wdown, units, padded)
    wait(parts)
    fill_gates(x, gate, dim, place[0], experts)
    for c, cols in enumerate(columns(dim)):
        wait(loads[c])

        def multiply(rows):
            product = nt(x[rows, cols], win[:, cols])
            hidden[rows, :] = product if c == 0 else hidden[rows, :] + product

        each_rows(rows_all, multiply)

    def pointwise(rows):
        g, u = hidden[rows, pl.ds(0, padded)], hidden[rows, pl.ds(padded, padded)]
        sig = jax.nn.sigmoid(g)
        gated = g * sig
        silu[rows, :] = gated
        slope[rows, :] = u * sig * (1.0 + g * (1.0 - sig))
        act[rows, :] = (gated * u).astype(BF16)

    each_rows(rows_all, pointwise)
    stores = []
    for c, cols in enumerate(columns(dim)):
        wait(down[c])

        def multiply(rows):
            part = nn(act[rows, :], wdown[:, cols]).astype(BF16)
            out[rows, cols] = (gate[rows, pl.ds(0, 1)] * part.astype(F32)).astype(BF16)

        each_rows(rows_all, multiply)
        pairs = [
            (out.at[pl.ds(half, half), cols], send.at[:, cols]),
            (out.at[pl.ds(0, half), cols], keep.at[:, cols]),
        ]
        stores.append(started(sems, base, pairs))
        base += 2
    for store in stores:
        wait(store)


def backward_kernel(
    experts, units, place, ya, yb, silu, slope, w_in, w_down, grad, keep, send,
    y, win, wdown, total, gate, out, sems,
):
    dim = w_down.shape[1]
    rows_all, half, padded = y.shape[0], y.shape[0] // 2, silu.shape[1]
    width = y.shape[1] - dim
    parts = started(sems, 0, two_halves(ya, yb, y, pl.ds(dim, width)))
    base, loads, wide = 2, [], []
    for cols in columns(dim):
        pairs = two_halves(ya, yb, y, cols)
        pairs.append((w_down.at[:, cols], wdown.at[pl.ds(0, units), cols]))
        loads.append(started(sems, base, pairs))
        base += len(pairs)
    for cols in columns(dim):
        wide.append(started(sems, base, in_pairs(w_in, win, units, padded, cols)))
        base += 2
    clear_pad(win, units, padded)
    clear_pad(wdown, units, padded)
    wait(parts)
    fill_gates(y, gate, dim, place[0], experts)
    for c, cols in enumerate(columns(dim)):
        wait(loads[c])

        def multiply(rows):
            scaled = (gate[rows, pl.ds(0, 1)] * y[rows, cols].astype(F32)).astype(BF16)
            product = nt(scaled, wdown[:, cols])
            total[rows, :] = product if c == 0 else total[rows, :] + product

        each_rows(rows_all, multiply)

    def pointwise(rows):
        value = total[rows, :]
        grad[rows, pl.ds(0, padded)] = (value * slope[rows, :]).astype(BF16)
        grad[rows, pl.ds(padded, padded)] = (value * silu[rows, :]).astype(BF16)

    each_rows(rows_all, pointwise)
    stores = []
    for c, cols in enumerate(columns(dim)):
        wait(wide[c])

        def multiply(rows):
            out[rows, cols] = nn(grad[rows, :], win[:, cols]).astype(BF16)

        each_rows(rows_all, multiply)
        pairs = [
            (out.at[pl.ds(half, half), cols], send.at[:, cols]),
            (out.at[pl.ds(0, half), cols], keep.at[:, cols]),
        ]
        stores.append(started(sems, base, pairs))
        base += 2
    for store in stores:
        wait(store)


def weight_kernel(experts, units, scaled, place, own, away, ra, rb, grads, r, gate, turned, out, sems):
    dim = grads.shape[2]
    groups = grads.shape[0]
    padded = own.shape[1] // groups
    rows_all = r.shape[0]
    width = r.shape[1] - dim
    base, loads, stores = 0, [], []
    if scaled:
        parts = started(sems, 0, two_halves(ra, rb, r, pl.ds(dim, width)))
        base = 2
    for cols in columns(dim):
        loads.append(started(sems, base, two_halves(ra, rb, r, cols)))
        base += 2

    def choose(rows):
        used = jnp.where(place[2] > 0, away[rows, :], own[rows, :])
        turned[:, rows] = used.T

    each_rows(rows_all, choose)
    if scaled:
        wait(parts)
        fill_gates(r, gate, dim, place[1], experts)
    for c, cols in enumerate(columns(dim)):
        wait(loads[c])
        if scaled:

            def scale(rows):
                r[rows, cols] = (gate[rows, pl.ds(0, 1)] * r[rows, cols].astype(F32)).astype(BF16)

            each_rows(rows_all, scale)
        pairs = []
        for i in range(groups):
            some = pl.ds(i * padded, units)
            out[some, cols] = nn(turned[some, :], r[:, cols]).astype(BF16)
            pairs.append((out.at[some, cols], grads.at[i, :, cols]))
        stores.append(started(sems, base, pairs))
        base += groups
    for store in stores:
        wait(store)


def rounded_up(value, unit):
    return -(-value // unit) * unit


def params(mib):
    return pltpu.CompilerParams(vmem_limit_bytes=mib * 1024 * 1024)


def cost(flops, size):
    return pl.CostEstimate(flops=flops, bytes_accessed=size, transcendentals=0)


def masks(axis):
    size, out = lax.axis_size(axis), []
    while size > 1:
        size //= 2
        out.append((axis, size))
    return out


def partner(block, bit):
    axis, mask = bit
    return lax.ppermute(block, axis, [(i, i ^ mask) for i in range(lax.axis_size(axis))])


def inner_rows(bit, done, order, unit):
    for other in done:
        if order.index(other) > order.index(bit):
            unit *= 2
    return unit


def join(a, b, inner):
    pair = [part.reshape(-1, inner, part.shape[-1]) for part in (a, b)]
    return jnp.concatenate(pair, axis=1).reshape(-1, a.shape[-1])


def halves(block, inner):
    split = block.reshape(-1, 2, inner, block.shape[1])
    return [split[:, i].reshape(-1, block.shape[1]) for i in (0, 1)]


def is_set(bit):
    return (lax.axis_index(bit[0]) & bit[1]) > 0


def add(a, b):
    return (a.astype(F32) + b.astype(F32)).astype(BF16)


def on_device(tokens, cotangent, gates, expert_ids, swap_flag, w_in, w_down):
    experts = lax.axis_size("expert")
    half_axis = experts // 2
    tok_dev, dim = tokens.shape
    me = lax.axis_index("expert")
    slots = jnp.arange(experts, dtype=jnp.int32)
    flag = jnp.sum(jnp.where(slots == me, swap_flag, 0))
    held = jnp.where(flag > 0, me ^ half_axis, me)
    place = jnp.stack([me, held, flag]).astype(jnp.int32)
    units = w_down.shape[1]
    padded = rounded_up(units, 128)
    my_in, my_down = w_in.reshape(2, units, dim), w_down.reshape(units, dim)

    across, within = masks("dp"), masks("expert")
    core, near, far = within[-1], within[-2:-1], within[:-2]
    first = near + across
    second = across + near
    order = first[::-1] + far[::-1]
    rows_all = tok_dev * lax.axis_size("dp") * experts

    dense = jnp.sum(
        jnp.where(expert_ids[:, :, None] == slots, gates[:, :, None], 0.0), axis=1
    )
    parts = jnp.concatenate(split_three(dense), axis=1)
    width = rounded_up(parts.shape[1], 128)
    parts = jnp.pad(parts, ((0, 0), (0, width - parts.shape[1])))
    block = jnp.stack(
        [jnp.concatenate([rows, parts], axis=1) for rows in (tokens, cotangent)]
    )

    top = far[0]
    for i in range(0, len(far), 2):
        group = far[i : i + 2]
        a = group[0]
        flat = block.reshape(-1, dim + width)

        def other(mask):
            return partner(flat, ("expert", mask)).reshape(block.shape)

        if len(group) == 2:
            b = group[1]
            fours = [block, other(b[1]), other(a[1]), other(a[1] | b[1])]
            pairs = [jnp.concatenate(fours[:2], axis=1), jnp.concatenate(fours[2:], axis=1)]
        else:
            pairs = [block, other(a[1])]
        if a == top:
            turn = is_set(top)
            pairs = [jnp.where(turn, pairs[1 - j], pairs[j]) for j in (0, 1)]
        block = jnp.concatenate(pairs, axis=1)
    far_rows = block.shape[1]

    def plane(rows, route):
        done = []
        for bit in route:
            inner = inner_rows(bit, done, order, far_rows)
            rows = join(rows, partner(rows, bit), inner)
            done.append(bit)
        return rows

    xa = plane(block[0], first)
    ya = plane(block[1], second)
    xb = partner(xa, core)
    yb = partner(ya, core)

    row_type = jax.ShapeDtypeStruct((rows_all // 2, dim), BF16)
    weights = [
        pltpu.VMEM((2 * padded, dim), BF16),
        pltpu.VMEM((padded, dim), BF16),
    ]
    row_buffer = pltpu.VMEM((rows_all, dim + width), BF16)
    gate_buffer = pltpu.VMEM((rows_all, 128), F32)
    out_buffer = pltpu.VMEM((rows_all, dim), BF16)
    size = 2 * dim * (3 * units + 2 * rows_all)
    flops = 6 * rows_all * units * dim
    small = 48 if rows_all > 512 else 24
    act, silu, slope, keep, send = pl.pallas_call(
        functools.partial(forward_kernel, experts, units),
        out_shape=[
            jax.ShapeDtypeStruct((rows_all, padded), BF16),
            jax.ShapeDtypeStruct((rows_all, padded), F32),
            jax.ShapeDtypeStruct((rows_all, padded), F32),
            row_type,
            row_type,
        ],
        in_specs=[SMEM, ANY, ANY, ANY, ANY],
        out_specs=[VMEM, VMEM, VMEM, ANY, ANY],
        scratch_shapes=[
            row_buffer,
            *weights,
            pltpu.VMEM((rows_all, 2 * padded), F32),
            gate_buffer,
            out_buffer,
            pltpu.SemaphoreType.DMA((2 + 7 * CHUNKS,)),
        ],
        compiler_params=params(small + 8),
        cost_estimate=cost(flops, size),
        name="forward",
    )(place, xa, xb, my_in, my_down)
    mixed_keep, mixed_send = keep, send
    grad, back_keep, back_send = pl.pallas_call(
        functools.partial(backward_kernel, experts, units),
        out_shape=[
            jax.ShapeDtypeStruct((rows_all, 2 * padded), BF16),
            row_type,
            row_type,
        ],
        in_specs=[SMEM, ANY, ANY, VMEM, VMEM, ANY, ANY],
        out_specs=[VMEM, ANY, ANY],
        scratch_shapes=[
            row_buffer,
            *weights,
            pltpu.VMEM((rows_all, padded), F32),
            gate_buffer,
            out_buffer,
            pltpu.SemaphoreType.DMA((2 + 7 * CHUNKS,)),
        ],
        compiler_params=params(small + 8),
        cost_estimate=cost(flops, size),
        name="backward",
    )(place, ya, yb, silu, slope, my_in, my_down)

    def scatter(keep, send, route):
        got = partner(send, core)
        left = list(order)
        for bit in route:
            left.remove(bit)
            inner = inner_rows(bit, left, order, tok_dev)
            kept, sent = [add(*pair) for pair in zip(halves(keep, inner), halves(got, inner))]
            got = partner(sent, bit)
            keep = kept
        keep = add(keep, got)
        for i in reversed(range(0, len(far), 2)):
            group = far[i : i + 2]
            a = group[0]
            inner = keep.shape[0] // 2
            pair = [keep[:inner], keep[inner:]]
            if a == top:
                turn = is_set(top)
                pair = [jnp.where(turn, pair[1 - j], pair[j]) for j in (0, 1)]
            if len(group) == 2:
                b = group[1]
                low = inner // 2
                mine, others = pair[0][:low], (
                    (pair[0][low:], b[1]),
                    (pair[1][:low], a[1]),
                    (pair[1][low:], a[1] | b[1]),
                )
            else:
                mine, others = pair[0], ((pair[1], a[1]),)
            total = mine.astype(F32)
            for rows, mask in others:
                total = total + partner(rows, ("expert", mask)).astype(F32)
            keep = total.astype(BF16)
        return keep

    far_act = partner(act, ("expert", half_axis))
    mixed = scatter(mixed_keep, mixed_send, first[::-1])
    far_grad = partner(grad, ("expert", half_axis))
    grad_tokens = scatter(back_keep, back_send, second[::-1])

    def weight_gradient(own, away, ra, rb, scaled, name):
        groups = own.shape[1] // padded
        return pl.pallas_call(
            functools.partial(weight_kernel, experts, units, scaled),
            out_shape=jax.ShapeDtypeStruct((groups, units, dim), BF16),
            in_specs=[SMEM, VMEM, VMEM, ANY, ANY],
            out_specs=ANY,
            scratch_shapes=[
                row_buffer,
                gate_buffer,
                pltpu.VMEM((groups * padded, rows_all), BF16),
                pltpu.VMEM((groups * padded, dim), BF16),
                pltpu.SemaphoreType.DMA((2 + (2 + groups) * CHUNKS,)),
            ],
            compiler_params=params(small + 8),
            cost_estimate=cost(
                2 * rows_all * groups * units * dim, 2 * dim * (groups * units + rows_all)
            ),
            name=name,
        )(place, own, away, ra, rb)

    new_down = weight_gradient(act, far_act, ya, yb, True, "grad_down")
    new_in = weight_gradient(grad, far_grad, xa, xb, False, "grad_in")
    return (mixed, grad_tokens, new_in.reshape(w_in.shape), new_down.reshape(w_down.shape))


def solution(mesh):
    rows = P(("dp", "expert"), None)
    w_in, w_down = P("expert", None, "dp", None), P("expert", "dp", None)
    return jax.shard_map(
        on_device,
        mesh=mesh,
        in_specs=(rows, rows, rows, rows, P(), w_in, w_down),
        out_specs=(rows, rows, w_in, w_down),
        check_vma=False,
    )
```

```python
import functools

import jax
import jax.numpy as jnp
from jax import lax
from jax.experimental import pallas as pl
from jax.experimental.pallas import tpu as pltpu
from jax.sharding import PartitionSpec as P

F32, BF16 = jnp.float32, jnp.bfloat16
ANY = pl.BlockSpec(memory_space=pl.ANY)
HBM = pl.BlockSpec(memory_space=pltpu.HBM)
SMEM = pl.BlockSpec(memory_space=pltpu.SMEM)
VMEM = pl.BlockSpec(memory_space=pltpu.VMEM)
CHUNKS = 4
ROW_BLOCK = 256


def split_three(x):
    high = x.astype(BF16)
    rest = x - high.astype(F32)
    middle = rest.astype(BF16)
    low = (rest - middle.astype(F32)).astype(BF16)
    return high, middle, low


def nt(a, b):
    return lax.dot_general(a, b, (((1,), (1,)), ((), ())), preferred_element_type=F32)


def nn(a, b):
    return jnp.dot(a, b, preferred_element_type=F32)


def each_rows(total, body):
    if total <= ROW_BLOCK:
        body(pl.ds(0, total))
    else:

        @pl.loop(0, total // ROW_BLOCK)
        def _(i):
            body(pl.ds(pl.multiple_of(i * ROW_BLOCK, ROW_BLOCK), ROW_BLOCK))


def columns(dim):
    step = dim // CHUNKS
    return [pl.ds(c * step, step) for c in range(CHUNKS)]


def started(sems, base, pairs):
    copies = [
        pltpu.make_async_copy(source, target, sems.at[base + i])
        for i, (source, target) in enumerate(pairs)
    ]
    for copy in copies:
        copy.start()
    return copies


def wait(copies):
    for copy in copies:
        copy.wait()


def two_halves(first, second, buffer, cols):
    half = first.shape[0]
    return [
        (first.at[:, cols], buffer.at[pl.ds(0, half), cols]),
        (second.at[:, cols], buffer.at[pl.ds(half, half), cols]),
    ]


def gate_column(parts, expert, experts):
    lane = lax.broadcasted_iota(jnp.int32, parts.shape, 1)
    values = parts.astype(F32)
    high, middle, low = (
        jnp.sum(jnp.where(lane == expert + i * experts, values, 0.0), axis=1, keepdims=True)
        for i in range(3)
    )
    return (low + middle) + high


def fill_gates(buffer, gate, dim, expert, experts):
    width = buffer.shape[1] - dim

    def body(rows):
        column = gate_column(buffer[rows, pl.ds(dim, width)], expert, experts)
        gate[rows, :] = jnp.broadcast_to(column, (column.shape[0], gate.shape[1]))

    each_rows(buffer.shape[0], body)


def in_pairs(w_in, buffer, units, cols):
    return [(w_in.at[i, :, cols], buffer.at[pl.ds(i * units, units), cols]) for i in (0, 1)]


def forward_kernel(
    experts, place, xa, xb, w_in, w_down, act, silu, slope, gate, gate_held, keep, send,
    x, win, wdown, hidden, rows_act, sems,
):
    units, dim = w_down.shape
    rows_all, half = x.shape[0], x.shape[0] // 2
    width = x.shape[1] - dim
    base, loads, down = 0, [], []
    for cols in columns(dim):
        pairs = two_halves(xa, xb, x, cols) + in_pairs(w_in, win, units, cols)
        loads.append(started(sems, base, pairs))
        base += len(pairs)
    parts = started(sems, base, two_halves(xa, xb, x, pl.ds(dim, width)))
    base += 2
    for cols in columns(dim):
        down.append(started(sems, base, [(w_down.at[:, cols], wdown.at[:, cols])]))
        base += 1
    for c, cols in enumerate(columns(dim)):
        wait(loads[c])

        def multiply(rows):
            product = nt(win[:, cols], x[rows, cols])
            hidden[:, rows] = product if c == 0 else hidden[:, rows] + product

        each_rows(rows_all, multiply)
    wait(parts)
    fill_gates(x, gate, dim, place[0], experts)

    def pointwise(rows):
        g, u = hidden[pl.ds(0, units), rows], hidden[pl.ds(units, units), rows]
        sig = jax.nn.sigmoid(g)
        gated = g * sig
        silu[:, rows] = gated
        slope[:, rows] = u * sig * (1.0 + g * (1.0 - sig))
        value = (gated * u).astype(BF16)
        act[:, rows] = value
        rows_act[rows, :] = value.T

    each_rows(rows_all, pointwise)
    for c, cols in enumerate(columns(dim)):
        wait(down[c])

        def multiply(start, target):
            def body(rows):
                mine = pl.ds(rows.start + start, rows.size)
                part = nn(rows_act[mine, :], wdown[:, cols]).astype(BF16)
                target[rows, cols] = (gate[mine, pl.ds(0, 1)] * part.astype(F32)).astype(BF16)

            return body

        both_halves(half, multiply, keep, send)
    fill_gates(x, gate_held, dim, place[1], experts)


def both_halves(half, body, keep, send):
    each_rows(half, body(half, send))
    each_rows(half, body(0, keep))


def backward_kernel(
    ya, yb, silu, slope, gate, w_in, w_down, grad, keep, send,
    y, win, wdown, total, rows_grad, sems,
):
    units, dim = w_down.shape
    rows_all, half = y.shape[0], y.shape[0] // 2
    base, loads, wide = 0, [], []
    for cols in columns(dim):
        pairs = two_halves(ya, yb, y, cols) + [(w_down.at[:, cols], wdown.at[:, cols])]
        loads.append(started(sems, base, pairs))
        base += len(pairs)
    for cols in columns(dim):
        wide.append(started(sems, base, in_pairs(w_in, win, units, cols)))
        base += 2
    for c, cols in enumerate(columns(dim)):
        wait(loads[c])

        def multiply(rows):
            scaled = (gate[rows, pl.ds(0, 1)] * y[rows, cols].astype(F32)).astype(BF16)
            product = nt(wdown[:, cols], scaled)
            total[:, rows] = product if c == 0 else total[:, rows] + product

        each_rows(rows_all, multiply)

    def pointwise(rows):
        value = total[:, rows]
        for i, factor in enumerate((slope, silu)):
            some = pl.ds(i * units, units)
            grad[some, rows] = (value * factor[:, rows]).astype(BF16)
        rows_grad[rows, :] = grad[:, rows].T

    each_rows(rows_all, pointwise)
    for c, cols in enumerate(columns(dim)):
        wait(wide[c])

        def multiply(start, target):
            def body(rows):
                mine = pl.ds(rows.start + start, rows.size)
                target[rows, cols] = nn(rows_grad[mine, :], win[:, cols]).astype(BF16)

            return body

        both_halves(half, multiply, keep, send)


def weight_kernel(scaled, place, own, away, gate, ra, rb, grads, r, used, out, sems):
    groups, units, dim = grads.shape
    rows_all = r.shape[0]
    base, loads, stores = 0, [], []
    for cols in columns(dim):
        loads.append(started(sems, base, two_halves(ra, rb, r, cols)))
        base += 2

    used[...] = jnp.where(place[2] > 0, away[...], own[...])
    for c, cols in enumerate(columns(dim)):
        wait(loads[c])
        if scaled:

            def scale(rows):
                r[rows, cols] = (gate[rows, pl.ds(0, 1)] * r[rows, cols].astype(F32)).astype(BF16)

            each_rows(rows_all, scale)
        pairs = []
        for i in range(groups):
            some = pl.ds(i * units, units)
            out[some, cols] = nn(used[some, :], r[:, cols]).astype(BF16)
            pairs.append((out.at[some, cols], grads.at[i, :, cols]))
        stores.append(started(sems, base, pairs))
        base += groups
    for store in stores:
        wait(store)


def rounded_up(value, unit):
    return -(-value // unit) * unit


def params(mib):
    return pltpu.CompilerParams(vmem_limit_bytes=mib * 1024 * 1024)


def cost(flops, size):
    return pl.CostEstimate(flops=flops, bytes_accessed=size, transcendentals=0)


def masks(axis):
    size, out = lax.axis_size(axis), []
    while size > 1:
        size //= 2
        out.append((axis, size))
    return out


def partner(block, bit):
    axis, mask = bit
    return lax.ppermute(block, axis, [(i, i ^ mask) for i in range(lax.axis_size(axis))])


def inner_rows(bit, done, order, unit):
    for other in done:
        if order.index(other) > order.index(bit):
            unit *= 2
    return unit


def join(a, b, inner):
    pair = [part.reshape(-1, inner, part.shape[-1]) for part in (a, b)]
    return jnp.concatenate(pair, axis=1).reshape(-1, a.shape[-1])


def halves(block, inner):
    split = block.reshape(-1, 2, inner, block.shape[1])
    return [split[:, i].reshape(-1, block.shape[1]) for i in (0, 1)]


def is_set(bit):
    return (lax.axis_index(bit[0]) & bit[1]) > 0


def add(a, b):
    return (a.astype(F32) + b.astype(F32)).astype(BF16)


def on_device(tokens, cotangent, gates, expert_ids, swap_flag, w_in, w_down):
    experts = lax.axis_size("expert")
    half_axis = experts // 2
    tok_dev, dim = tokens.shape
    me = lax.axis_index("expert")
    slots = jnp.arange(experts, dtype=jnp.int32)
    flag = jnp.sum(jnp.where(slots == me, swap_flag, 0))
    held = jnp.where(flag > 0, me ^ half_axis, me)
    place = jnp.stack([me, held, flag]).astype(jnp.int32)
    units = w_down.shape[1]
    my_in, my_down = w_in.reshape(2, units, dim), w_down.reshape(units, dim)

    across, within = masks("dp"), masks("expert")
    core, near, far = within[-1], within[-2:-1], within[:-2]
    first = near + across
    second = across + near
    order = first[::-1] + far[::-1]
    rows_all = tok_dev * lax.axis_size("dp") * experts
    top = far[0]

    dense = jnp.sum(
        jnp.where(expert_ids[:, :, None] == slots, gates[:, :, None], 0.0), axis=1
    )
    parts = jnp.concatenate(split_three(dense), axis=1)
    width = rounded_up(parts.shape[1], 128)
    parts = jnp.pad(parts, ((0, 0), (0, width - parts.shape[1])))

    def far_gather(block):
        for i in range(0, len(far), 2):
            group = far[i : i + 2]
            a = group[0]
            if len(group) == 2:
                b = group[1]
                fours = [
                    block,
                    partner(block, b),
                    partner(block, a),
                    partner(block, ("expert", a[1] | b[1])),
                ]
                pairs = [jnp.concatenate(fours[:2]), jnp.concatenate(fours[2:])]
            else:
                pairs = [block, partner(block, a)]
            if a == top:
                turn = is_set(top)
                pairs = [jnp.where(turn, pairs[1 - j], pairs[j]) for j in (0, 1)]
            block = jnp.concatenate(pairs)
        return block

    def plane(rows, route):
        done, far_rows = [], rows.shape[0]
        for bit in route:
            inner = inner_rows(bit, done, order, far_rows)
            rows = join(rows, partner(rows, bit), inner)
            done.append(bit)
        return rows

    x_far = far_gather(jnp.concatenate([tokens, parts], axis=1))
    x_far, cotangent = lax.optimization_barrier((x_far, cotangent))
    y_far = far_gather(cotangent)
    xa = plane(x_far, first)
    ya = plane(y_far, second)
    xb = partner(xa, core)
    yb = partner(ya, core)

    row_type = jax.ShapeDtypeStruct((rows_all // 2, dim), BF16)
    weights = [pltpu.VMEM((2 * units, dim), BF16), pltpu.VMEM((units, dim), BF16)]
    gate_type = jax.ShapeDtypeStruct((rows_all, 128), F32)
    size = 2 * dim * (3 * units + 2 * rows_all)
    flops = 6 * rows_all * units * dim
    limit = 56 if rows_all > 512 else 32
    act, silu, slope, gate, gate_held, mixed_keep, mixed_send = pl.pallas_call(
        functools.partial(forward_kernel, experts),
        out_shape=[
            jax.ShapeDtypeStruct((units, rows_all), BF16),
            jax.ShapeDtypeStruct((units, rows_all), F32),
            jax.ShapeDtypeStruct((units, rows_all), F32),
            gate_type,
            gate_type,
            row_type,
            row_type,
        ],
        in_specs=[SMEM, ANY, ANY, HBM, HBM],
        out_specs=[VMEM] * 7,
        scratch_shapes=[
            pltpu.VMEM((rows_all, dim + width), BF16),
            *weights,
            pltpu.VMEM((2 * units, rows_all), F32),
            pltpu.VMEM((rows_all, units), BF16),
            pltpu.SemaphoreType.DMA((2 + 5 * CHUNKS,)),
        ],
        compiler_params=params(limit),
        cost_estimate=cost(flops, size),
        name="forward",
    )(place, xa, xb, my_in, my_down)
    grad, back_keep, back_send = pl.pallas_call(
        backward_kernel,
        out_shape=[
            jax.ShapeDtypeStruct((2 * units, rows_all), BF16),
            row_type,
            row_type,
        ],
        in_specs=[ANY, ANY, VMEM, VMEM, VMEM, HBM, HBM],
        out_specs=[VMEM] * 3,
        scratch_shapes=[
            pltpu.VMEM((rows_all, dim), BF16),
            *weights,
            pltpu.VMEM((units, rows_all), F32),
            pltpu.VMEM((rows_all, 2 * units), BF16),
            pltpu.SemaphoreType.DMA((5 * CHUNKS,)),
        ],
        compiler_params=params(limit),
        cost_estimate=cost(flops, size),
        name="backward",
    )(ya, yb, silu, slope, gate, my_in, my_down)

    def scatter(keep, send, route, marks):
        got = partner(send, core)
        left = list(order)
        for bit in route:
            left.remove(bit)
            inner = inner_rows(bit, left, order, tok_dev)
            kept, sent = [add(*pair) for pair in zip(halves(keep, inner), halves(got, inner))]
            marks.append(sent)
            got = partner(sent, bit)
            keep = kept
        keep = add(keep, got)
        for i in reversed(range(0, len(far), 2)):
            group = far[i : i + 2]
            a = group[0]
            inner = keep.shape[0] // 2
            pair = [keep[:inner], keep[inner:]]
            if a == top:
                turn = is_set(top)
                pair = [jnp.where(turn, pair[1 - j], pair[j]) for j in (0, 1)]
            if len(group) == 2:
                b = group[1]
                low = inner // 2
                mine, others = (
                    pair[0][:low],
                    (
                        (pair[0][low:], b[1]),
                        (pair[1][:low], a[1]),
                        (pair[1][low:], a[1] | b[1]),
                    ),
                )
            else:
                mine, others = pair[0], ((pair[1], a[1]),)
            total = mine.astype(F32)
            for rows, mask in others:
                total = total + partner(rows, ("expert", mask)).astype(F32)
            keep = total.astype(BF16)
        return keep

    mixed_marks, back_marks = [], []
    far_act = partner(act, ("expert", half_axis))
    mixed = scatter(mixed_keep, mixed_send, first[::-1], mixed_marks)
    far_grad = partner(grad, ("expert", half_axis))
    grad_tokens = scatter(back_keep, back_send, second[::-1], back_marks)

    def weight_gradient(after, own, away, ra, rb, scaled, name):
        groups = own.shape[0] // units
        here, _ = lax.optimization_barrier((place, after))
        return pl.pallas_call(
            functools.partial(weight_kernel, scaled),
            out_shape=jax.ShapeDtypeStruct((groups, units, dim), BF16),
            in_specs=[SMEM, VMEM, VMEM, VMEM, ANY, ANY],
            out_specs=ANY,
            scratch_shapes=[
                pltpu.VMEM((rows_all, dim), BF16),
                pltpu.VMEM(own.shape, BF16),
                pltpu.VMEM((groups * units, dim), BF16),
                pltpu.SemaphoreType.DMA(((2 + groups) * CHUNKS,)),
            ],
            compiler_params=params(limit),
            cost_estimate=cost(
                2 * rows_all * groups * units * dim, 2 * dim * (groups * units + rows_all)
            ),
            name=name,
        )(here, own, away, gate_held, ra, rb)

    new_down = weight_gradient((mixed_marks[-1], back_marks[0]), act, far_act, ya, yb, True, "grad_down")
    new_in = weight_gradient(back_marks[-1], grad, far_grad, xa, xb, False, "grad_in")
    return (mixed, grad_tokens, new_in.reshape(w_in.shape), new_down.reshape(w_down.shape))


def solution(mesh):
    rows = P(("dp", "expert"), None)
    w_in, w_down = P("expert", None, "dp", None), P("expert", "dp", None)
    return jax.shard_map(
        on_device,
        mesh=mesh,
        in_specs=(rows, rows, rows, rows, P(), w_in, w_down),
        out_specs=(rows, rows, w_in, w_down),
        check_vma=False,
    )
```

```python
import functools

import jax
import jax.numpy as jnp
from jax import lax
from jax.experimental import pallas as pl
from jax.experimental.pallas import tpu as pltpu
from jax.sharding import PartitionSpec as P

F32, BF16 = jnp.float32, jnp.bfloat16
ANY = pl.BlockSpec(memory_space=pl.ANY)
SMEM = pl.BlockSpec(memory_space=pltpu.SMEM)
VMEM = pl.BlockSpec(memory_space=pltpu.VMEM)
CHUNKS = 4
ROW_BLOCK = 256


def split_three(x):
    high = x.astype(BF16)
    rest = x - high.astype(F32)
    middle = rest.astype(BF16)
    low = (rest - middle.astype(F32)).astype(BF16)
    return high, middle, low


def nt(a, b):
    return lax.dot_general(a, b, (((1,), (1,)), ((), ())), preferred_element_type=F32)


def nn(a, b):
    return jnp.dot(a, b, preferred_element_type=F32)


def each_rows(total, body):
    if total <= ROW_BLOCK:
        body(pl.ds(0, total))
    else:

        @pl.loop(0, total // ROW_BLOCK)
        def _(i):
            body(pl.ds(pl.multiple_of(i * ROW_BLOCK, ROW_BLOCK), ROW_BLOCK))


def columns(dim):
    step = dim // CHUNKS
    return [pl.ds(c * step, step) for c in range(CHUNKS)]


def started(sems, base, pairs):
    copies = [
        pltpu.make_async_copy(source, target, sems.at[base + i])
        for i, (source, target) in enumerate(pairs)
    ]
    for copy in copies:
        copy.start()
    return copies


def wait(copies):
    for copy in copies:
        copy.wait()


def row_copies(pieces, buffer, cols):
    half, left = pieces[0].shape
    out = []
    for i, piece in enumerate(pieces):
        low, high = (0, left) if i % 2 == 0 else (left, left + piece.shape[1])
        if low <= cols.start and cols.start + cols.size <= high:
            source = piece.at[:, pl.ds(cols.start - low, cols.size)]
            out.append((source, buffer.at[pl.ds(i // 2 * half, half), cols]))
    return out


def gate_column(parts, expert, experts):
    lane = lax.broadcasted_iota(jnp.int32, parts.shape, 1)
    values = parts.astype(F32)
    high, middle, low = (
        jnp.sum(jnp.where(lane == expert + i * experts, values, 0.0), axis=1, keepdims=True)
        for i in range(3)
    )
    return (low + middle) + high


def fill_gates(buffer, gate, dim, expert, experts):
    width = buffer.shape[1] - dim

    def body(rows):
        column = gate_column(buffer[rows, pl.ds(dim, width)], expert, experts)
        gate[rows, :] = jnp.broadcast_to(column, (column.shape[0], gate.shape[1]))

    each_rows(buffer.shape[0], body)


def held_expert(flags):
    me = lax.axis_index("expert")
    flag = flags[me]
    return me, jnp.where(flag > 0, me ^ (lax.axis_size("expert") // 2), me), flag


def stage_kernel(after, rows, w_in, w_down, rows_out, in_out, down_out, sems):
    pairs = []
    for c, cols in enumerate(columns(w_in.shape[1])):
        pairs += [(w_in.at[:, cols], in_out.at[:, cols]), (w_down.at[:, cols], down_out.at[:, cols])]
    wait(started(sems, 0, pairs))


def forward_kernel(
    experts, flags, x0, x1, x2, x3, win, wdown, act, silu, slope, gate, gate_held,
    keep0, keep1, send0, send1, x, hidden, rows_act, sems,
):
    units, dim = wdown.shape
    rows_all, half = x.shape[0], x.shape[0] // 2
    pieces = (x0, x1, x2, x3)
    base, loads = 0, []
    for cols in columns(dim) + [pl.ds(dim, x.shape[1] - dim)]:
        loads.append(started(sems, base, row_copies(pieces, x, cols)))
        base += 2
    for c, cols in enumerate(columns(dim)):
        wait(loads[c])

        def multiply(rows):
            product = nt(win[:, cols], x[rows, cols])
            hidden[:, rows] = product if c == 0 else hidden[:, rows] + product

        each_rows(rows_all, multiply)
    wait(loads[-1])
    me, held, _ = held_expert(flags)
    fill_gates(x, gate, dim, me, experts)

    def pointwise(rows):
        g, u = hidden[pl.ds(0, units), rows], hidden[pl.ds(units, units), rows]
        sig = jax.nn.sigmoid(g)
        gated = g * sig
        silu[:, rows] = gated
        slope[:, rows] = u * sig * (1.0 + g * (1.0 - sig))
        value = (gated * u).astype(BF16)
        act[:, rows] = value
        rows_act[rows, :] = value.T

    each_rows(rows_all, pointwise)
    for c, cols in enumerate(columns(dim)):

        def multiply(start, target, cols=cols):
            out = pl.ds(cols.start % (dim // 2), cols.size)

            def body(rows):
                mine = pl.ds(rows.start + start, rows.size)
                part = nn(rows_act[mine, :], wdown[:, cols]).astype(BF16)
                target[rows, out] = (gate[mine, pl.ds(0, 1)] * part.astype(F32)).astype(BF16)

            return body

        side = c * 2 // CHUNKS
        each_rows(half, multiply(half, (send0, send1)[side]))
        each_rows(half, multiply(0, (keep0, keep1)[side]))
    fill_gates(x, gate_held, dim, held, experts)


def backward_kernel(
    y0, y1, y2, y3, silu, slope, gate, win, wdown, grad,
    keep0, keep1, send0, send1, y, total, rows_grad, sems,
):
    units, dim = wdown.shape
    rows_all, half = y.shape[0], y.shape[0] // 2
    pieces = (y0, y1, y2, y3)
    base, loads = 0, []
    for cols in columns(dim):
        loads.append(started(sems, base, row_copies(pieces, y, cols)))
        base += 2
    for c, cols in enumerate(columns(dim)):
        wait(loads[c])

        def multiply(rows):
            scaled = (gate[rows, pl.ds(0, 1)] * y[rows, cols].astype(F32)).astype(BF16)
            product = nt(wdown[:, cols], scaled)
            total[:, rows] = product if c == 0 else total[:, rows] + product

        each_rows(rows_all, multiply)

    def pointwise(rows):
        value = total[:, rows]
        for i, factor in enumerate((slope, silu)):
            some = pl.ds(i * units, units)
            grad[some, rows] = (value * factor[:, rows]).astype(BF16)
        rows_grad[rows, :] = grad[:, rows].T

    each_rows(rows_all, pointwise)
    for c, cols in enumerate(columns(dim)):

        def multiply(start, target, cols=cols):
            out = pl.ds(cols.start % (dim // 2), cols.size)

            def body(rows):
                mine = pl.ds(rows.start + start, rows.size)
                target[rows, out] = nn(rows_grad[mine, :], win[:, cols]).astype(BF16)

            return body

        side = c * 2 // CHUNKS
        each_rows(half, multiply(half, (send0, send1)[side]))
        each_rows(half, multiply(0, (keep0, keep1)[side]))


def weight_kernel(
    scaled, flags, own, away, gate, r0, r1, r2, r3, *rest
):
    grads, r, used, out, sems = rest[-5:]
    groups, units, dim = grads.shape
    rows_all = r.shape[0]
    base, loads, stores = 0, [], []
    for cols in columns(dim):
        loads.append(started(sems, base, row_copies((r0, r1, r2, r3), r, cols)))
        base += 2
    _, _, flag = held_expert(flags)
    used[...] = jnp.where(flag > 0, away[...], own[...])
    for c, cols in enumerate(columns(dim)):
        wait(loads[c])
        if scaled:

            def scale(rows):
                r[rows, cols] = (gate[rows, pl.ds(0, 1)] * r[rows, cols].astype(F32)).astype(BF16)

            each_rows(rows_all, scale)
        pairs = []
        for i in range(groups):
            some = pl.ds(i * units, units)
            out[some, cols] = nn(used[some, :], r[:, cols]).astype(BF16)
            pairs.append((out.at[some, cols], grads.at[i, :, cols]))
        stores.append(started(sems, base, pairs))
        base += groups
    for store in stores:
        wait(store)


def rounded_up(value, unit):
    return -(-value // unit) * unit


def params(mib):
    return pltpu.CompilerParams(vmem_limit_bytes=mib * 1024 * 1024)


def cost(flops, size):
    return pl.CostEstimate(flops=flops, bytes_accessed=size, transcendentals=0)


def masks(axis):
    size, out = lax.axis_size(axis), []
    while size > 1:
        size //= 2
        out.append((axis, size))
    return out


def partner(block, bit):
    axis, mask = bit
    return lax.ppermute(block, axis, [(i, i ^ mask) for i in range(lax.axis_size(axis))])


def inner_rows(bit, done, order, unit):
    for other in done:
        if order.index(other) > order.index(bit):
            unit *= 2
    return unit


def join(a, b, inner):
    pair = [part.reshape(-1, inner, part.shape[-1]) for part in (a, b)]
    return jnp.concatenate(pair, axis=1).reshape(-1, a.shape[-1])


def halves(block, inner):
    split = block.reshape(-1, 2, inner, block.shape[1])
    return [split[:, i].reshape(-1, block.shape[1]) for i in (0, 1)]


def is_set(bit):
    return (lax.axis_index(bit[0]) & bit[1]) > 0


def add(a, b):
    return (a.astype(F32) + b.astype(F32)).astype(BF16)


def on_device(tokens, cotangent, gates, expert_ids, swap_flag, w_in, w_down):
    experts = lax.axis_size("expert")
    half_axis = experts // 2
    tok_dev, dim = tokens.shape
    slots = jnp.arange(experts, dtype=jnp.int32)
    units = w_down.shape[1]

    across, within = masks("dp"), masks("expert")
    core, near, far = within[-1], within[-2:-1], within[:-2]
    first = near + across
    second = across + near
    order = first[::-1] + far[::-1]
    rows_all = tok_dev * lax.axis_size("dp") * experts
    top = far[0]

    dense = jnp.sum(
        jnp.where(expert_ids[:, :, None] == slots, gates[:, :, None], 0.0), axis=1
    )
    parts = jnp.concatenate(split_three(dense), axis=1)
    width = rounded_up(parts.shape[1], 128)
    parts = jnp.pad(parts, ((0, 0), (0, width - parts.shape[1])))

    def far_gather(block, seen):
        for i in range(0, len(far), 2):
            group = far[i : i + 2]
            a = group[0]
            if len(group) == 2:
                b = group[1]
                fours = [
                    block,
                    partner(block, b),
                    partner(block, a),
                    partner(block, ("expert", a[1] | b[1])),
                ]
                seen.append(fours[1])
                pairs = [jnp.concatenate(fours[:2]), jnp.concatenate(fours[2:])]
            else:
                pairs = [block, partner(block, a)]
                seen.append(pairs[1])
            if a == top:
                turn = is_set(top)
                pairs = [jnp.where(turn, pairs[1 - j], pairs[j]) for j in (0, 1)]
            block = jnp.concatenate(pairs)
        return block

    def plane(rows, route):
        done, far_rows = [], rows.shape[0]
        for bit in route:
            inner = inner_rows(bit, done, order, far_rows)
            rows = join(rows, partner(rows, bit), inner)
            done.append(bit)
        return rows

    def gathered(block):
        own = [plane(block[:, : dim // 2], first), plane(block[:, dim // 2 :], second)]
        return own + [partner(piece, core) for piece in own]

    seen = []
    payload = jnp.concatenate([tokens, parts], axis=1)
    x_far = far_gather(payload, seen)
    cotangent, win, wdown = pl.pallas_call(
        stage_kernel,
        out_shape=[
            jax.ShapeDtypeStruct(cotangent.shape, BF16),
            jax.ShapeDtypeStruct((2 * units, dim), BF16),
            jax.ShapeDtypeStruct((units, dim), BF16),
        ],
        in_specs=[ANY] * 4,
        out_specs=[ANY, VMEM, VMEM],
        scratch_shapes=[pltpu.SemaphoreType.DMA((2 * CHUNKS,))],
        input_output_aliases={1: 0},
        compiler_params=params(40),
        cost_estimate=cost(0, 12 * units * dim),
        name="stage",
    )(seen[0], cotangent, w_in.reshape(2 * units, dim), w_down.reshape(units, dim))
    y_far = far_gather(cotangent, seen)
    xs = gathered(x_far)
    ys = gathered(y_far)

    row_type = jax.ShapeDtypeStruct((rows_all // 2, dim // 2), BF16)
    gate_type = jax.ShapeDtypeStruct((rows_all, 128), F32)
    size = 2 * dim * (3 * units + 2 * rows_all)
    flops = 6 * rows_all * units * dim
    limit = 60 if rows_all > 512 else 24
    act, silu, slope, gate, gate_held, *mixed_rows = pl.pallas_call(
        functools.partial(forward_kernel, experts),
        out_shape=[
            jax.ShapeDtypeStruct((units, rows_all), BF16),
            jax.ShapeDtypeStruct((units, rows_all), F32),
            jax.ShapeDtypeStruct((units, rows_all), F32),
            gate_type,
            gate_type,
            *[row_type] * 4,
        ],
        in_specs=[SMEM] + [ANY] * 4 + [VMEM] * 2,
        out_specs=[VMEM] * 9,
        scratch_shapes=[
            pltpu.VMEM((rows_all, dim + width), BF16),
            pltpu.VMEM((2 * units, rows_all), F32),
            pltpu.VMEM((rows_all, units), BF16),
            pltpu.SemaphoreType.DMA((2 + 2 * CHUNKS,)),
        ],
        compiler_params=params(limit),
        cost_estimate=cost(flops, size),
        name="forward",
    )(swap_flag, *xs, win, wdown)
    grad, *back_rows = pl.pallas_call(
        backward_kernel,
        out_shape=[
            jax.ShapeDtypeStruct((2 * units, rows_all), BF16),
            *[row_type] * 4,
        ],
        in_specs=[ANY] * 4 + [VMEM] * 5,
        out_specs=[VMEM] * 5,
        scratch_shapes=[
            pltpu.VMEM((rows_all, dim), BF16),
            pltpu.VMEM((units, rows_all), F32),
            pltpu.VMEM((rows_all, 2 * units), BF16),
            pltpu.SemaphoreType.DMA((2 * CHUNKS,)),
        ],
        compiler_params=params(limit),
        cost_estimate=cost(flops, size),
        name="backward",
    )(*ys, silu, slope, gate, win, wdown)

    def plane_sum(keep, got, route, marks):
        left = list(order)
        for bit in route:
            left.remove(bit)
            inner = inner_rows(bit, left, order, tok_dev)
            kept, sent = [add(*pair) for pair in zip(halves(keep, inner), halves(got, inner))]
            marks.append(sent)
            got = partner(sent, bit)
            keep = kept
        return add(keep, got)

    def scatter(parts, marks):
        got = [partner(send, core) for send in parts[2:]]
        routes = first[::-1], second[::-1]
        sums = [plane_sum(*side, marks) for side in zip(parts[:2], got, routes)]
        keep = jnp.concatenate(sums, axis=1)
        for i in reversed(range(0, len(far), 2)):
            group = far[i : i + 2]
            a = group[0]
            inner = keep.shape[0] // 2
            pair = [keep[:inner], keep[inner:]]
            if a == top:
                turn = is_set(top)
                pair = [jnp.where(turn, pair[1 - j], pair[j]) for j in (0, 1)]
            if len(group) == 2:
                b = group[1]
                low = inner // 2
                mine, others = (
                    pair[0][:low],
                    (
                        (pair[0][low:], b[1]),
                        (pair[1][:low], a[1]),
                        (pair[1][low:], a[1] | b[1]),
                    ),
                )
            else:
                mine, others = pair[0], ((pair[1], a[1]),)
            total = mine.astype(F32)
            arrived = [partner(rows, ("expert", mask)) for rows, mask in others]
            marks.append(arrived[0])
            for rows in arrived:
                total = total + rows.astype(F32)
            keep = total.astype(BF16)
        return keep

    mixed_marks, back_marks = [], []
    far_act = partner(act, ("expert", half_axis))
    mixed = scatter(mixed_rows, mixed_marks)
    far_grad = partner(grad, ("expert", half_axis))
    grad_tokens = scatter(back_rows, back_marks)

    def weight_gradient(after, own, away, pieces, scaled, name):
        groups = own.shape[0] // units
        return pl.pallas_call(
            functools.partial(weight_kernel, scaled),
            out_shape=jax.ShapeDtypeStruct((groups, units, dim), BF16),
            in_specs=[SMEM] + [VMEM] * 3 + [ANY] * (4 + len(after)),
            out_specs=ANY,
            scratch_shapes=[
                pltpu.VMEM((rows_all, dim), BF16),
                pltpu.VMEM(own.shape, BF16),
                pltpu.VMEM((groups * units, dim), BF16),
                pltpu.SemaphoreType.DMA(((2 + groups) * CHUNKS,)),
            ],
            compiler_params=params(limit),
            cost_estimate=cost(
                2 * rows_all * groups * units * dim, 2 * dim * (groups * units + rows_all)
            ),
            name=name,
        )(swap_flag, own, away, gate_held, *pieces, *after)

    new_down = weight_gradient((back_marks[0], back_marks[len(near + across)]), act, far_act, ys, True, "grad_down")
    new_in = weight_gradient(back_marks[-1:], grad, far_grad, xs, False, "grad_in")
    return (mixed, grad_tokens, new_in.reshape(w_in.shape), new_down.reshape(w_down.shape))


def solution(mesh):
    rows = P(("dp", "expert"), None)
    w_in, w_down = P("expert", None, "dp", None), P("expert", "dp", None)
    return jax.shard_map(
        on_device,
        mesh=mesh,
        in_specs=(rows, rows, rows, rows, P(), w_in, w_down),
        out_specs=(rows, rows, w_in, w_down),
        check_vma=False,
    )
```

```python
import functools

import jax
import jax.numpy as jnp
from jax import lax
from jax.experimental import pallas as pl
from jax.experimental.pallas import tpu as pltpu
from jax.sharding import PartitionSpec as P

F32, BF16 = jnp.float32, jnp.bfloat16
ANY = pl.BlockSpec(memory_space=pl.ANY)
SMEM = pl.BlockSpec(memory_space=pltpu.SMEM)
VMEM = pl.BlockSpec(memory_space=pltpu.VMEM)
CHUNKS = 4
ROW_BLOCK = 256
STAGE_MIB = 40


def split_three(x):
    high = x.astype(BF16)
    rest = x - high.astype(F32)
    middle = rest.astype(BF16)
    low = (rest - middle.astype(F32)).astype(BF16)
    return high, middle, low


def nt(a, b):
    return lax.dot_general(a, b, (((1,), (1,)), ((), ())), preferred_element_type=F32)


def nn(a, b):
    return jnp.dot(a, b, preferred_element_type=F32)


def each_rows(total, body):
    if total <= ROW_BLOCK:
        body(pl.ds(0, total))
    else:

        @pl.loop(0, total // ROW_BLOCK)
        def _(i):
            body(pl.ds(pl.multiple_of(i * ROW_BLOCK, ROW_BLOCK), ROW_BLOCK))


def columns(dim):
    step = dim // CHUNKS
    return [pl.ds(c * step, step) for c in range(CHUNKS)]


def started(sems, base, pairs):
    copies = [
        pltpu.make_async_copy(source, target, sems.at[base + i])
        for i, (source, target) in enumerate(pairs)
    ]
    for copy in copies:
        copy.start()
    return copies


def wait(copies):
    for copy in copies:
        copy.wait()


def row_copies(own, other, buffer, cols):
    half = own.shape[0]
    return [
        (own.at[:, cols], buffer.at[pl.ds(0, half), cols]),
        (other.at[:, cols], buffer.at[pl.ds(half, half), cols]),
    ]


def gate_column(parts, expert, experts):
    lane = lax.broadcasted_iota(jnp.int32, parts.shape, 1)
    values = parts.astype(F32)
    high, middle, low = (
        jnp.sum(jnp.where(lane == expert + i * experts, values, 0.0), axis=1, keepdims=True)
        for i in range(3)
    )
    return (low + middle) + high


def fill_gates(buffer, gate, dim, expert, experts):
    width = buffer.shape[1] - dim

    def body(rows):
        column = gate_column(buffer[rows, pl.ds(dim, width)], expert, experts)
        gate[rows, :] = jnp.broadcast_to(column, (column.shape[0], gate.shape[1]))

    each_rows(buffer.shape[0], body)


def held_expert(flags):
    near, core = (lax.axis_size(axis) for axis in ("near", "core"))
    half = lax.axis_size("far") * near * core // 2
    me = (lax.axis_index("far") * near + lax.axis_index("near")) * core + lax.axis_index("core")
    flag = flags[me]
    return me, jnp.where(flag > 0, (me + half) % (2 * half), me), flag


def stage_kernel(after, rows, weight, rows_out, out, sems):
    pairs = [(weight.at[:, cols], out.at[:, cols]) for cols in columns(weight.shape[1])]
    wait(started(sems, 0, pairs))


def forward_kernel(
    experts, flags, xa, xb, win, wdown, act, silu, slope, gate, gate_held,
    keep, send, x, hidden, rows_act, sems,
):
    units, dim = wdown.shape
    rows_all, half = x.shape[0], x.shape[0] // 2
    base, loads = 0, []
    for cols in columns(dim) + [pl.ds(dim, x.shape[1] - dim)]:
        loads.append(started(sems, base, row_copies(xa, xb, x, cols)))
        base += 2
    for c, cols in enumerate(columns(dim)):
        wait(loads[c])

        def multiply(rows):
            product = nt(win[:, cols], x[rows, cols])
            hidden[:, rows] = product if c == 0 else hidden[:, rows] + product

        each_rows(rows_all, multiply)
    wait(loads[-1])
    me, held, _ = held_expert(flags)
    fill_gates(x, gate, dim, me, experts)

    def pointwise(rows):
        g, u = hidden[pl.ds(0, units), rows], hidden[pl.ds(units, units), rows]
        sig = jax.nn.sigmoid(g)
        gated = g * sig
        silu[:, rows] = gated
        slope[:, rows] = u * sig * (1.0 + g * (1.0 - sig))
        value = (gated * u).astype(BF16)
        act[:, rows] = value
        rows_act[rows, :] = value.T

    each_rows(rows_all, pointwise)
    for c, cols in enumerate(columns(dim)):

        def multiply(start, target):
            def body(rows):
                mine = pl.ds(rows.start + start, rows.size)
                part = nn(rows_act[mine, :], wdown[:, cols]).astype(BF16)
                target[rows, cols] = (gate[mine, pl.ds(0, 1)] * part.astype(F32)).astype(BF16)

            return body

        each_rows(half, multiply(half, send))
        each_rows(half, multiply(0, keep))
    fill_gates(x, gate_held, dim, held, experts)


def backward_kernel(
    ya, yb, silu, slope, gate, win, wdown, grad,
    keep, send, y, total, rows_grad, sems,
):
    units, dim = wdown.shape
    rows_all, half = y.shape[0], y.shape[0] // 2
    base, loads = 0, []
    for cols in columns(dim):
        loads.append(started(sems, base, row_copies(ya, yb, y, cols)))
        base += 2
    for c, cols in enumerate(columns(dim)):
        wait(loads[c])

        def multiply(rows):
            scaled = (gate[rows, pl.ds(0, 1)] * y[rows, cols].astype(F32)).astype(BF16)
            product = nt(wdown[:, cols], scaled)
            total[:, rows] = product if c == 0 else total[:, rows] + product

        each_rows(rows_all, multiply)

    def pointwise(rows):
        value = total[:, rows]
        for i, factor in enumerate((slope, silu)):
            some = pl.ds(i * units, units)
            grad[some, rows] = (value * factor[:, rows]).astype(BF16)
        rows_grad[rows, :] = grad[:, rows].T

    each_rows(rows_all, pointwise)
    for c, cols in enumerate(columns(dim)):

        def multiply(start, target):
            def body(rows):
                mine = pl.ds(rows.start + start, rows.size)
                target[rows, cols] = nn(rows_grad[mine, :], win[:, cols]).astype(BF16)

            return body

        each_rows(half, multiply(half, send))
        each_rows(half, multiply(0, keep))


def weight_kernel(
    scaled, flags, own, away, gate, ra, rb, *rest
):
    grads, r, used, out, sems = rest[-5:]
    groups, units, dim = grads.shape
    rows_all = r.shape[0]
    base, loads, stores = 0, [], []
    for cols in columns(dim):
        loads.append(started(sems, base, row_copies(ra, rb, r, cols)))
        base += 2
    _, _, flag = held_expert(flags)
    used[...] = jnp.where(flag > 0, away[...], own[...])
    for c, cols in enumerate(columns(dim)):
        wait(loads[c])
        if scaled:

            def scale(rows):
                r[rows, cols] = (gate[rows, pl.ds(0, 1)] * r[rows, cols].astype(F32)).astype(BF16)

            each_rows(rows_all, scale)
        pairs = []
        for i in range(groups):
            some = pl.ds(i * units, units)
            out[some, cols] = nn(used[some, :], r[:, cols]).astype(BF16)
            pairs.append((out.at[some, cols], grads.at[i, :, cols]))
        stores.append(started(sems, base, pairs))
        base += groups
    for store in stores:
        wait(store)


def rounded_up(value, unit):
    return -(-value // unit) * unit


def params(mib):
    return pltpu.CompilerParams(vmem_limit_bytes=mib * 1024 * 1024)


def cost(flops, size):
    return pl.CostEstimate(flops=flops, bytes_accessed=size, transcendentals=0)


def other(block, axis):
    size = lax.axis_size(axis)
    return lax.ppermute(block, axis, [(i, (i + size // 2) % size) for i in range(size)])


def gather(rows, axes):
    size = lax.axis_size(axes)
    copies = jnp.broadcast_to(rows[None], (size, *rows.shape))
    return lax.all_to_all(copies, axes, 0, 0).reshape(-1, rows.shape[1])


def scatter_sum(rows, axes):
    size = lax.axis_size(axes)
    parts = lax.all_to_all(rows.reshape(size, -1, rows.shape[1]), axes, 0, 0)
    return parts, jnp.sum(parts.astype(F32), axis=0).astype(BF16)


def add(a, b):
    return (a.astype(F32) + b.astype(F32)).astype(BF16)


def on_device(tokens, cotangent, gates, expert_ids, swap_flag, w_in, w_down):
    experts = swap_flag.shape[0]
    tok_dev, dim = tokens.shape
    slots = jnp.arange(experts, dtype=jnp.int32)
    units = w_down.shape[1]
    rows_all = tok_dev * lax.axis_size("dp") * experts
    plane = ("dp", "near")

    dense = jnp.sum(
        jnp.where(expert_ids[:, :, None] == slots, gates[:, :, None], 0.0), axis=1
    )
    parts = jnp.concatenate(split_three(dense), axis=1)
    width = rounded_up(parts.shape[1], 128)
    parts = jnp.pad(parts, ((0, 0), (0, width - parts.shape[1])))
    payload = jnp.concatenate([tokens, parts], axis=1)

    def stage(after, rows, weight, name):
        return pl.pallas_call(
            stage_kernel,
            out_shape=[
                jax.ShapeDtypeStruct(rows.shape, rows.dtype),
                jax.ShapeDtypeStruct(weight.shape, BF16),
            ],
            in_specs=[ANY] * 3,
            out_specs=[ANY, VMEM],
            scratch_shapes=[pltpu.SemaphoreType.DMA((CHUNKS,))],
            input_output_aliases={1: 0},
            compiler_params=params(STAGE_MIB),
            cost_estimate=cost(0, 4 * weight.size),
            name=name,
        )(after, rows, weight)

    x_far = gather(payload, "far")
    cotangent, win = stage(payload, cotangent, w_in.reshape(2 * units, dim), "stage_in")
    cotangent, wdown = stage(x_far, cotangent, w_down.reshape(units, dim), "stage_down")
    y_far = gather(cotangent, "far")
    xa = gather(x_far, plane)
    ya = gather(y_far, plane)
    xs = xa, other(xa, "core")
    ys = ya, other(ya, "core")

    row_type = jax.ShapeDtypeStruct((rows_all // 2, dim), BF16)
    gate_type = jax.ShapeDtypeStruct((rows_all, 128), F32)
    size = 2 * dim * (3 * units + 2 * rows_all)
    flops = 6 * rows_all * units * dim
    limit = 60 if rows_all > 512 else 24
    act, silu, slope, gate, gate_held, *mixed_rows = pl.pallas_call(
        functools.partial(forward_kernel, experts),
        out_shape=[
            jax.ShapeDtypeStruct((units, rows_all), BF16),
            jax.ShapeDtypeStruct((units, rows_all), F32),
            jax.ShapeDtypeStruct((units, rows_all), F32),
            gate_type,
            gate_type,
            row_type,
            row_type,
        ],
        in_specs=[SMEM] + [ANY] * 2 + [VMEM] * 2,
        out_specs=[VMEM] * 7,
        scratch_shapes=[
            pltpu.VMEM((rows_all, dim + width), BF16),
            pltpu.VMEM((2 * units, rows_all), F32),
            pltpu.VMEM((rows_all, units), BF16),
            pltpu.SemaphoreType.DMA((2 + 2 * CHUNKS,)),
        ],
        compiler_params=params(limit),
        cost_estimate=cost(flops, size),
        name="forward",
    )(swap_flag, *xs, win, wdown)
    grad, *back_rows = pl.pallas_call(
        backward_kernel,
        out_shape=[
            jax.ShapeDtypeStruct((2 * units, rows_all), BF16),
            row_type,
            row_type,
        ],
        in_specs=[ANY] * 2 + [VMEM] * 5,
        out_specs=[VMEM] * 3,
        scratch_shapes=[
            pltpu.VMEM((rows_all, dim), BF16),
            pltpu.VMEM((units, rows_all), F32),
            pltpu.VMEM((rows_all, 2 * units), BF16),
            pltpu.SemaphoreType.DMA((2 * CHUNKS,)),
        ],
        compiler_params=params(limit),
        cost_estimate=cost(flops, size),
        name="backward",
    )(*ys, silu, slope, gate, win, wdown)

    def scatter(keep, send):
        rows = add(keep, other(send, "core"))
        parts, some = scatter_sum(rows, plane)
        return rows, parts, scatter_sum(some, "far")[1]

    far_act = other(act, "far")
    mixed_whole, _, mixed = scatter(*mixed_rows)
    far_grad = other(grad, "far")
    back_whole, back_parts, grad_tokens = scatter(*back_rows)

    def weight_gradient(after, own, away, pieces, scaled, name):
        groups = own.shape[0] // units
        return pl.pallas_call(
            functools.partial(weight_kernel, scaled),
            out_shape=jax.ShapeDtypeStruct((groups, units, dim), BF16),
            in_specs=[SMEM] + [VMEM] * 3 + [ANY] * 3,
            out_specs=ANY,
            scratch_shapes=[
                pltpu.VMEM((rows_all, dim), BF16),
                pltpu.VMEM(own.shape, BF16),
                pltpu.VMEM((groups * units, dim), BF16),
                pltpu.SemaphoreType.DMA(((2 + groups) * CHUNKS,)),
            ],
            compiler_params=params(limit),
            cost_estimate=cost(
                2 * rows_all * groups * units * dim, 2 * dim * (groups * units + rows_all)
            ),
            name=name,
        )(swap_flag, own, away, gate_held, *pieces, after)

    new_down = weight_gradient(back_whole, act, far_act, ys, True, "grad_down")
    new_in = weight_gradient(back_parts, grad, far_grad, xs, False, "grad_in")
    return (mixed, grad_tokens, new_in.reshape(w_in.shape), new_down.reshape(w_down.shape))


def solution(mesh):
    dp, experts = mesh.shape["dp"], mesh.shape["expert"]
    split = jax.sharding.Mesh(
        mesh.devices.reshape(dp, experts // 4, 2, 2), ("dp", "far", "near", "core")
    )
    expert = ("far", "near", "core")
    rows = P(("dp", *expert), None)
    w_in, w_down = P(expert, None, "dp", None), P(expert, "dp", None)
    return jax.shard_map(
        on_device,
        mesh=split,
        in_specs=(rows, rows, rows, rows, P(), w_in, w_down),
        out_specs=(rows, rows, w_in, w_down),
        check_vma=False,
    )
```

```python
import functools

import jax
import jax.numpy as jnp
from jax import lax
from jax.experimental import pallas as pl
from jax.experimental.pallas import tpu as pltpu
from jax.sharding import PartitionSpec as P

F32, BF16 = jnp.float32, jnp.bfloat16
ANY = pl.BlockSpec(memory_space=pl.ANY)
SMEM = pl.BlockSpec(memory_space=pltpu.SMEM)
VMEM = pl.BlockSpec(memory_space=pltpu.VMEM)
CHUNKS = 4
ROW_BLOCK = 256
STAGE_MIB = 40


def nt(a, b):
    return lax.dot_general(a, b, (((1,), (1,)), ((), ())), preferred_element_type=F32)


def nn(a, b):
    return jnp.dot(a, b, preferred_element_type=F32)


def each_rows(total, body):
    if total <= ROW_BLOCK:
        body(pl.ds(0, total))
    else:

        @pl.loop(0, total // ROW_BLOCK)
        def _(i):
            body(pl.ds(pl.multiple_of(i * ROW_BLOCK, ROW_BLOCK), ROW_BLOCK))


def columns(dim):
    step = dim // CHUNKS
    return [pl.ds(c * step, step) for c in range(CHUNKS)]


def started(sems, base, pairs):
    copies = [
        pltpu.make_async_copy(source, target, sems.at[base + i])
        for i, (source, target) in enumerate(pairs)
    ]
    for copy in copies:
        copy.start()
    return copies


def wait(copies):
    for copy in copies:
        copy.wait()


def row_copies(own, received, buffer, cols, target=None):
    half = own.shape[0]
    target = cols if target is None else target
    return [
        (own.at[:, cols], buffer.at[pl.ds(0, half), target]),
        (received.at[:, cols], buffer.at[pl.ds(half, half), target]),
    ]


def split_three(x):
    high = x.astype(BF16)
    rest = x - high.astype(F32)
    middle = rest.astype(BF16)
    low = (rest - middle.astype(F32)).astype(BF16)
    return high, middle, low


def gate_column(parts, expert, experts):
    lane = lax.broadcasted_iota(jnp.int32, parts.shape, 1)
    values = parts.astype(F32)
    high, middle, low = (
        jnp.sum(jnp.where(lane == expert + i * experts, values, 0.0), axis=1, keepdims=True)
        for i in range(3)
    )
    return (low + middle) + high


def fill_gates(parts, gate, expert, experts):
    def body(rows):
        column = gate_column(parts[rows, :], expert, experts)
        gate[rows, :] = jnp.broadcast_to(column, (column.shape[0], gate.shape[1]))

    each_rows(parts.shape[0], body)


def held_expert(flags):
    me = lax.axis_index("expert")
    flag = flags[me]
    return me, jnp.where(flag > 0, me ^ (lax.axis_size("expert") // 2), me), flag


def zero_kernel(*refs):
    refs[-1][...] = jnp.zeros_like(refs[-1])


def stage_kernel(after, weight, out, sems):
    wait(started(sems, 0, [(weight.at[:, c], out.at[:, c]) for c in columns(weight.shape[1])]))


def hidden_kernel(xa, xb, win, after, act, silu, slope, zero, x, hidden, sems):
    units, rows_all = act.shape
    dim = win.shape[1]
    loads = []
    for c, cols in enumerate(columns(dim)):
        loads.append(started(sems, 2 * c, row_copies(xa, xb, x, cols)))
    zero[...] = jnp.zeros_like(zero)
    for c, cols in enumerate(columns(dim)):
        wait(loads[c])

        def multiply(rows):
            product = nt(win[:, cols], x[rows, cols])
            hidden[:, rows] = product if c == 0 else hidden[:, rows] + product

        each_rows(rows_all, multiply)

    def pointwise(rows):
        g, u = hidden[pl.ds(0, units), rows], hidden[pl.ds(units, units), rows]
        sig = jax.nn.sigmoid(g)
        gated = g * sig
        silu[:, rows] = gated
        slope[:, rows] = u * sig * (1.0 + g * (1.0 - sig))
        act[:, rows] = (gated * u).astype(BF16)

    each_rows(rows_all, pointwise)


def split_product(rows_ref, weight, keep0, keep1, send, finish):
    half, dim = send.shape
    for c, cols in enumerate(columns(dim)):
        keep = (keep0, keep1)[c * 2 // CHUNKS]
        inner = pl.ds(cols.start % (dim // 2), cols.size)

        def multiply(start, target, place):
            def body(rows):
                mine = pl.ds(rows.start + start, rows.size)
                target[rows, place] = finish(mine, nn(rows_ref[mine, :], weight[:, cols]).astype(BF16))

            return body

        each_rows(half, multiply(half, send, cols))
        each_rows(half, multiply(0, keep, inner))


def part_kernel(
    experts, flags, xa, xb, act, wdown, after, keep0, keep1, send, gate, gate_held,
    parts, rows_act, sems,
):
    dim, width = wdown.shape[1], parts.shape[1]
    rows_all = parts.shape[0]
    loads = started(sems, 0, row_copies(xa, xb, parts, pl.ds(dim, width), pl.ds(0, width)))

    def turn(rows):
        rows_act[rows, :] = act[:, rows].T

    each_rows(rows_all, turn)
    me, held, _ = held_expert(flags)
    wait(loads)
    fill_gates(parts, gate, me, experts)
    fill_gates(parts, gate_held, held, experts)

    def weighted(rows, part):
        return (gate[rows, pl.ds(0, 1)] * part.astype(F32)).astype(BF16)

    split_product(rows_act, wdown, keep0, keep1, send, weighted)


def factor_kernel(ya, yb, silu, slope, gate, wdown, after, grad, y, total, sems):
    units, dim = wdown.shape
    rows_all = y.shape[0]
    loads = []
    for c, cols in enumerate(columns(dim)):
        loads.append(started(sems, 2 * c, row_copies(ya, yb, y, cols)))
    for c, cols in enumerate(columns(dim)):
        wait(loads[c])

        def multiply(rows):
            scaled = (gate[rows, pl.ds(0, 1)] * y[rows, cols].astype(F32)).astype(BF16)
            product = nt(wdown[:, cols], scaled)
            total[:, rows] = product if c == 0 else total[:, rows] + product

        each_rows(rows_all, multiply)

    def pointwise(rows):
        value = total[:, rows]
        for i, factor in enumerate((slope, silu)):
            grad[pl.ds(i * units, units), rows] = (value * factor[:, rows]).astype(BF16)

    each_rows(rows_all, pointwise)


def back_kernel(grad, win, keep0, keep1, send, rows_grad):
    def turn(rows):
        rows_grad[rows, :] = grad[:, rows].T

    each_rows(rows_grad.shape[0], turn)
    split_product(rows_grad, win, keep0, keep1, send, lambda rows, part: part)


def weight_kernel(
    scaled, flags, own, away, gate, ra, rb, *rest
):
    grads, r, used, out, sems = rest[-5:]
    groups, units, dim = grads.shape
    rows_all = r.shape[0]
    base, loads, stores = 0, [], []
    for cols in columns(dim):
        loads.append(started(sems, base, row_copies(ra, rb, r, cols)))
        base += 2
    _, _, flag = held_expert(flags)
    used[...] = jnp.where(flag > 0, away[...], own[...])
    for c, cols in enumerate(columns(dim)):
        wait(loads[c])
        if scaled:

            def scale(rows):
                r[rows, cols] = (gate[rows, pl.ds(0, 1)] * r[rows, cols].astype(F32)).astype(BF16)

            each_rows(rows_all, scale)
        pairs = []
        for i in range(groups):
            some = pl.ds(i * units, units)
            out[some, cols] = nn(used[some, :], r[:, cols]).astype(BF16)
            pairs.append((out.at[some, cols], grads.at[i, :, cols]))
        stores.append(started(sems, base, pairs))
        base += groups
    for store in stores:
        wait(store)


def rounded_up(value, unit):
    return -(-value // unit) * unit


def params(mib):
    return pltpu.CompilerParams(vmem_limit_bytes=mib * 1024 * 1024)


def cost(flops, size):
    return pl.CostEstimate(flops=flops, bytes_accessed=size, transcendentals=0)


def masks(axis):
    size, out = lax.axis_size(axis), []
    while size > 1:
        size //= 2
        out.append((axis, size))
    return out


def partner(block, bit):
    axis, mask = bit
    return lax.ppermute(block, axis, [(i, i ^ mask) for i in range(lax.axis_size(axis))])


def inner_rows(bit, done, order, unit):
    for other in done:
        if order.index(other) > order.index(bit):
            unit *= 2
    return unit


def join(a, b, inner):
    pair = [part.reshape(-1, inner, part.shape[-1]) for part in (a, b)]
    return jnp.concatenate(pair, axis=1).reshape(-1, a.shape[-1])


def halves(block, inner):
    split = block.reshape(-1, 2, inner, block.shape[1])
    return [split[:, i].reshape(-1, block.shape[1]) for i in (0, 1)]


def is_set(bit):
    return (lax.axis_index(bit[0]) & bit[1]) > 0


def add(a, b):
    return (a.astype(F32) + b.astype(F32)).astype(BF16)


def on_device(tokens, cotangent, gates, expert_ids, swap_flag, w_in, w_down):
    experts = lax.axis_size("expert")
    half_axis = experts // 2
    tok_dev, dim = tokens.shape
    units = w_down.shape[1]

    across, within = masks("dp"), masks("expert")
    core, near, far = within[-1], within[-2:-1], within[:-2]
    first = near + across
    second = across + near
    order = first[::-1] + far[::-1]
    rows_all = tok_dev * lax.axis_size("dp") * experts
    top = far[0]

    slots = jnp.arange(experts, dtype=jnp.int32)
    dense = jnp.sum(
        jnp.where(expert_ids[:, :, None] == slots, gates[:, :, None], 0.0), axis=1
    )
    parts = jnp.concatenate(split_three(dense), axis=1)
    width = rounded_up(parts.shape[1], 128)
    parts = jnp.pad(parts, ((0, 0), (0, width - parts.shape[1])))
    payload = jnp.concatenate([tokens, parts], axis=1)

    def far_gather(block, seen):
        for i in range(0, len(far), 2):
            group = far[i : i + 2]
            a = group[0]
            if len(group) == 2:
                b = group[1]
                fours = [
                    block,
                    partner(block, b),
                    partner(block, a),
                    partner(block, ("expert", a[1] | b[1])),
                ]
                seen.append(fours[1])
                pairs = [jnp.concatenate(fours[:2]), jnp.concatenate(fours[2:])]
            else:
                pairs = [block, partner(block, a)]
                seen.append(pairs[1])
            if a == top:
                turn = is_set(top)
                pairs = [jnp.where(turn, pairs[1 - j], pairs[j]) for j in (0, 1)]
            block = jnp.concatenate(pairs)
        return block

    def zero_after(*arrays):
        return pl.pallas_call(
            zero_kernel,
            out_shape=jax.ShapeDtypeStruct((16, dim // 2), BF16),
            in_specs=[ANY] * len(arrays),
            out_specs=VMEM,
            compiler_params=params(2),
            name="zero",
        )(*arrays)[:1]

    def plane_steps(block, zero=None):
        sides = [block[:, : dim // 2], block[:, dim // 2 :]]
        steps = []
        for k in range(len(first)):
            for i, route in enumerate((first, second)):
                bit = route[k]
                inner = inner_rows(bit, route[:k], order, far_rows)
                got = partner(sides[i], bit)
                if zero is not None and k == len(first) - 1:
                    got = got + zero()
                sides[i] = join(sides[i], got, inner)
            steps.append(list(sides))
        return steps

    def stage(after, weight, name):
        return pl.pallas_call(
            stage_kernel,
            out_shape=jax.ShapeDtypeStruct(weight.shape, BF16),
            in_specs=[ANY] * 2,
            out_specs=VMEM,
            scratch_shapes=[pltpu.SemaphoreType.DMA((CHUNKS,))],
            compiler_params=params(STAGE_MIB),
            cost_estimate=cost(0, 4 * weight.size),
            name=name,
        )(after, weight)

    seen = []
    x_far = far_gather(payload, seen)
    win = stage(seen[0], w_in.reshape(2 * units, dim), "stage_in")
    wdown = stage(seen[0], w_down.reshape(units, dim), "stage_down")
    far_rows = x_far.shape[0]
    x_steps = plane_steps(x_far)
    row = zero_after(x_steps[0][0])
    y_far = far_gather(cotangent + jnp.concatenate([row, row], axis=1), seen)
    xa = jnp.concatenate(x_steps[-1], axis=1)
    xb = partner(xa, core)

    half_rows = rows_all // 2
    limit = 60 if rows_all > 512 else 24
    rows_out = [
        jax.ShapeDtypeStruct((half_rows, dim // 2), BF16),
        jax.ShapeDtypeStruct((half_rows, dim // 2), BF16),
        jax.ShapeDtypeStruct((half_rows, dim), BF16),
    ]
    gate_type = jax.ShapeDtypeStruct((rows_all, 128), F32)
    saved_type = jax.ShapeDtypeStruct((units, rows_all), F32)
    product = 2 * rows_all * units * dim
    act, silu, slope, zero = pl.pallas_call(
        hidden_kernel,
        out_shape=[
            jax.ShapeDtypeStruct((units, rows_all), BF16),
            saved_type,
            saved_type,
            jax.ShapeDtypeStruct((16, dim // 2), BF16),
        ],
        in_specs=[ANY, ANY, VMEM, ANY],
        out_specs=[VMEM] * 4,
        scratch_shapes=[
            pltpu.VMEM((rows_all, dim), BF16),
            pltpu.VMEM((2 * units, rows_all), F32),
            pltpu.SemaphoreType.DMA((2 * CHUNKS,)),
        ],
        compiler_params=params(limit),
        cost_estimate=cost(2 * product, 4 * dim * (units + rows_all)),
        name="hidden",
    )(xa, xb, win, wdown)
    far_act = partner(act, ("expert", half_axis))
    ya = jnp.concatenate(plane_steps(y_far, lambda: zero[:1])[-1], axis=1)
    yb = partner(ya, core)
    *mixed_rows, gate, gate_held = pl.pallas_call(
        functools.partial(part_kernel, experts),
        out_shape=[*rows_out, gate_type, gate_type],
        in_specs=[SMEM, ANY, ANY, VMEM, VMEM, ANY],
        out_specs=[VMEM] * 5,
        scratch_shapes=[
            pltpu.VMEM((rows_all, width), BF16),
            pltpu.VMEM((rows_all, units), BF16),
            pltpu.SemaphoreType.DMA((2,)),
        ],
        compiler_params=params(limit),
        cost_estimate=cost(product, 2 * dim * (units + rows_all)),
        name="part",
    )(swap_flag, xa, xb, act, wdown, ya)
    grad = pl.pallas_call(
        factor_kernel,
        out_shape=jax.ShapeDtypeStruct((2 * units, rows_all), BF16),
        in_specs=[ANY] * 2 + [VMEM] * 4 + [ANY],
        out_specs=VMEM,
        scratch_shapes=[
            pltpu.VMEM((rows_all, dim), BF16),
            pltpu.VMEM((units, rows_all), F32),
            pltpu.SemaphoreType.DMA((2 * CHUNKS,)),
        ],
        compiler_params=params(limit),
        cost_estimate=cost(product, 2 * dim * (units + rows_all)),
        name="factors",
    )(ya, yb, silu, slope, gate, wdown, mixed_rows[2])
    far_grad = partner(grad, ("expert", half_axis))
    back_rows = pl.pallas_call(
        back_kernel,
        out_shape=rows_out,
        in_specs=[VMEM] * 2,
        out_specs=[VMEM] * 3,
        scratch_shapes=[pltpu.VMEM((rows_all, 2 * units), BF16)],
        compiler_params=params(limit),
        cost_estimate=cost(2 * product, 4 * dim * (units + rows_all)),
        name="back",
    )(grad, win)

    def added(keep, got, bit, left):
        inner = inner_rows(bit, left, order, tok_dev)
        return [add(*pair) for pair in zip(halves(keep, inner), halves(got, inner))]

    def far_sends(keep, groups):
        group = groups[-1]
        a = group[0]
        inner = keep.shape[0] // 2
        pair = [keep[:inner], keep[inner:]]
        if a == top:
            turn = is_set(top)
            pair = [jnp.where(turn, pair[1 - j], pair[j]) for j in (0, 1)]
        if len(group) == 1:
            return pair[0], [(pair[1], a[1])]
        b = group[1]
        low = inner // 2
        return pair[0][:low], [
            (pair[0][low:], b[1]),
            (pair[1][:low], a[1]),
            (pair[1][low:], a[1] | b[1]),
        ]

    def far_sum(mine, sends):
        arrived = [partner(rows, ("expert", mask)) for rows, mask in sends]
        total = mine.astype(F32)
        for rows in arrived:
            total = total + rows.astype(F32)
        return total.astype(BF16), arrived[0]

    groups = [far[i : i + 2] for i in range(0, len(far), 2)]
    routes = first[::-1], second[::-1]

    def core_sum(parts):
        got = partner(parts[2], core)
        return [parts[0], parts[1]], [got[:, : dim // 2], got[:, dim // 2 :]]

    keeps, gots = zip(core_sum(mixed_rows), core_sum(back_rows))
    sent = [None, None]
    zero = None
    for k in range(len(first)):
        for n in (0, 1):
            sent[n] = []
            for i, route in enumerate(routes):
                got = gots[n][i] if zero is None or n else gots[n][i] + zero
                left = set(order) - set(route[: k + 1])
                keeps[n][i], out = added(keeps[n][i], got, route[k], left)
                sent[n].append(out)
            for i, route in enumerate(routes):
                gots[n][i] = partner(sent[n][i], route[k])
        zero = zero_after(*sent[1])

    def plane_end(n, zero):
        return jnp.concatenate(
            [add(keep, got + zero) for keep, got in zip(keeps[n], gots[n])], axis=1
        )

    mine, sends = far_sends(plane_end(0, zero), groups)
    zero = zero_after(*[rows for rows, _ in sends])
    mixed, _ = far_sum(mine, sends)
    mine, sends = far_sends(plane_end(1, zero), groups)
    behind = [rows for rows, _ in sends]
    grad_tokens, back_near = far_sum(mine, sends)
    for group in groups[-2::-1]:
        mixed, _ = far_sum(*far_sends(mixed, [group]))
        grad_tokens, back_near = far_sum(*far_sends(grad_tokens, [group]))

    def weight_gradient(after, own, away, pieces, scaled, name):
        groups = own.shape[0] // units
        return pl.pallas_call(
            functools.partial(weight_kernel, scaled),
            out_shape=jax.ShapeDtypeStruct((groups, units, dim), BF16),
            in_specs=[SMEM] + [VMEM] * 3 + [ANY] * (2 + len(after)),
            out_specs=ANY,
            scratch_shapes=[
                pltpu.VMEM((rows_all, dim), BF16),
                pltpu.VMEM(own.shape, BF16),
                pltpu.VMEM((groups * units, dim), BF16),
                pltpu.SemaphoreType.DMA(((2 + groups) * CHUNKS,)),
            ],
            compiler_params=params(limit),
            cost_estimate=cost(
                2 * rows_all * groups * units * dim, 2 * dim * (groups * units + rows_all)
            ),
            name=name,
        )(swap_flag, own, away, gate_held, *pieces, *after)

    new_down = weight_gradient(behind, act, far_act, (ya, yb), True, "grad_down")
    new_in = weight_gradient([back_near], grad, far_grad, (xa, xb), False, "grad_in")
    return (mixed, grad_tokens, new_in.reshape(w_in.shape), new_down.reshape(w_down.shape))


def solution(mesh):
    rows = P(("dp", "expert"), None)
    w_in, w_down = P("expert", None, "dp", None), P("expert", "dp", None)
    return jax.shard_map(
        on_device,
        mesh=mesh,
        in_specs=(rows, rows, rows, rows, P(), w_in, w_down),
        out_specs=(rows, rows, w_in, w_down),
        check_vma=False,
    )
```

```python
import functools

import jax
import jax.numpy as jnp
from jax import lax
from jax.experimental import pallas as pl
from jax.experimental.pallas import tpu as pltpu
from jax.sharding import PartitionSpec as P

F32, BF16 = jnp.float32, jnp.bfloat16
ANY = pl.BlockSpec(memory_space=pl.ANY)
SMEM = pl.BlockSpec(memory_space=pltpu.SMEM)
VMEM = pl.BlockSpec(memory_space=pltpu.VMEM)
CHUNKS = 4
ROW_BLOCK = 256
STAGE_MIB = 40


def nt(a, b):
    return lax.dot_general(a, b, (((1,), (1,)), ((), ())), preferred_element_type=F32)


def nn(a, b):
    return jnp.dot(a, b, preferred_element_type=F32)


def each_rows(total, body):
    if total <= ROW_BLOCK:
        body(pl.ds(0, total))
    else:

        @pl.loop(0, total // ROW_BLOCK)
        def _(i):
            body(pl.ds(pl.multiple_of(i * ROW_BLOCK, ROW_BLOCK), ROW_BLOCK))


def columns(dim):
    step = dim // CHUNKS
    return [pl.ds(c * step, step) for c in range(CHUNKS)]


def started(sems, base, pairs):
    copies = [
        pltpu.make_async_copy(source, target, sems.at[base + i])
        for i, (source, target) in enumerate(pairs)
    ]
    for copy in copies:
        copy.start()
    return copies


def wait(copies):
    for copy in copies:
        copy.wait()


def row_copies(own, received, buffer, cols, target=None):
    half = own.shape[0]
    target = cols if target is None else target
    return [
        (own.at[:, cols], buffer.at[pl.ds(0, half), target]),
        (received.at[:, cols], buffer.at[pl.ds(half, half), target]),
    ]


def split_three(x):
    high = x.astype(BF16)
    rest = x - high.astype(F32)
    middle = rest.astype(BF16)
    low = (rest - middle.astype(F32)).astype(BF16)
    return high, middle, low


def gate_column(parts, expert, experts):
    lane = lax.broadcasted_iota(jnp.int32, parts.shape, 1)
    values = parts.astype(F32)
    high, middle, low = (
        jnp.sum(jnp.where(lane == expert + i * experts, values, 0.0), axis=1, keepdims=True)
        for i in range(3)
    )
    return (low + middle) + high


def fill_gates(parts, gate, expert, experts):
    def body(rows):
        column = gate_column(parts[rows, :], expert, experts)
        gate[rows, :] = jnp.broadcast_to(column, (column.shape[0], gate.shape[1]))

    each_rows(parts.shape[0], body)


def held_expert(flags):
    me = lax.axis_index("expert")
    flag = flags[me]
    return me, jnp.where(flag > 0, me ^ (lax.axis_size("expert") // 2), me), flag


def stage_kernel(after, weight, out, sems):
    wait(started(sems, 0, [(weight.at[:, c], out.at[:, c]) for c in columns(weight.shape[1])]))


def zero_kernel(*refs):
    refs[-1][...] = jnp.zeros_like(refs[-1])


def hidden_kernel(xa, xb, win, after, act, silu, slope, x, hidden, sems):
    units, rows_all = act.shape
    dim = win.shape[1]
    loads = []
    for c, cols in enumerate(columns(dim)):
        loads.append(started(sems, 2 * c, row_copies(xa, xb, x, cols)))
    for c, cols in enumerate(columns(dim)):
        wait(loads[c])

        def multiply(rows):
            product = nt(win[:, cols], x[rows, cols])
            hidden[:, rows] = product if c == 0 else hidden[:, rows] + product

        each_rows(rows_all, multiply)

    def pointwise(rows):
        g, u = hidden[pl.ds(0, units), rows], hidden[pl.ds(units, units), rows]
        sig = jax.nn.sigmoid(g)
        gated = g * sig
        silu[:, rows] = gated
        slope[:, rows] = u * sig * (1.0 + g * (1.0 - sig))
        act[:, rows] = (gated * u).astype(BF16)

    each_rows(rows_all, pointwise)


def split_product(rows_ref, weight, keep, send, cols, to, finish):
    half = send.shape[0]

    def multiply(start, target, place):
        def body(rows):
            mine = pl.ds(rows.start + start, rows.size)
            target[rows, place] = finish(mine, nn(rows_ref[mine, :], weight[:, cols]).astype(BF16))

        return body

    each_rows(half, multiply(half, send, to))
    each_rows(half, multiply(0, keep, cols))


def output_kernel(
    gate, factors, win, wdown, mixed, back, send, rows_act, rows_grad
):
    units, dim = wdown.shape

    def turn(rows):
        rows_act[rows, :] = factors[pl.ds(0, units), rows].T
        rows_grad[rows, :] = factors[pl.ds(units, 2 * units), rows].T

    def weighted(rows, part):
        return (gate[rows, pl.ds(0, 1)] * part.astype(F32)).astype(BF16)

    each_rows(rows_act.shape[0], turn)
    for cols in columns(dim):
        split_product(rows_act, wdown, mixed, send, cols, cols, weighted)
    for cols in columns(dim):
        to = pl.ds(dim + cols.start, cols.size)
        split_product(rows_grad, win, back, send, cols, to, lambda rows, part: part)


def factor_kernel(
    experts, flags, xa, xb, ya, yb, act, silu, slope, wdown, factors, gate, gate_held,
    y, total, parts, sems,
):
    units, dim = wdown.shape
    rows_all, width = parts.shape
    loads = []
    gates = started(sems, 0, row_copies(xa, xb, parts, pl.ds(dim, width), pl.ds(0, width)))
    for c, cols in enumerate(columns(dim)):
        loads.append(started(sems, 2 + 2 * c, row_copies(ya, yb, y, cols)))
    factors[pl.ds(0, units), :] = act[...]
    me, held, _ = held_expert(flags)
    wait(gates)
    fill_gates(parts, gate, me, experts)
    for c, cols in enumerate(columns(dim)):
        wait(loads[c])

        def multiply(rows):
            scaled = (gate[rows, pl.ds(0, 1)] * y[rows, cols].astype(F32)).astype(BF16)
            product = nt(wdown[:, cols], scaled)
            total[:, rows] = product if c == 0 else total[:, rows] + product

        each_rows(rows_all, multiply)

    def pointwise(rows):
        value = total[:, rows]
        factors[pl.ds(units, units), rows] = (value * slope[:, rows]).astype(BF16)
        factors[pl.ds(2 * units, units), rows] = (value * silu[:, rows]).astype(BF16)

    each_rows(rows_all, pointwise)
    fill_gates(parts, gate_held, held, experts)


def weight_kernel(first, scaled, flags, own, away, gate, ra, rb, *rest):
    grads, r, used, out, sems = rest[-5:]
    groups, units, dim = grads.shape
    rows_all = r.shape[0]
    base, loads, stores = 0, [], []
    for cols in columns(dim):
        loads.append(started(sems, base, row_copies(ra, rb, r, cols)))
        base += 2
    _, _, flag = held_expert(flags)
    some = pl.ds(first * units, groups * units)
    used[...] = jnp.where(flag > 0, away[some, :], own[some, :])
    for c, cols in enumerate(columns(dim)):
        wait(loads[c])
        if scaled:

            def scale(rows):
                r[rows, cols] = (gate[rows, pl.ds(0, 1)] * r[rows, cols].astype(F32)).astype(BF16)

            each_rows(rows_all, scale)
        pairs = []
        for i in range(groups):
            some = pl.ds(i * units, units)
            out[some, cols] = nn(used[some, :], r[:, cols]).astype(BF16)
            pairs.append((out.at[some, cols], grads.at[i, :, cols]))
        stores.append(started(sems, base, pairs))
        base += groups
    for store in stores:
        wait(store)


def rounded_up(value, unit):
    return -(-value // unit) * unit


def params(mib):
    return pltpu.CompilerParams(vmem_limit_bytes=mib * 1024 * 1024)


def cost(flops, size):
    return pl.CostEstimate(flops=flops, bytes_accessed=size, transcendentals=0)


def masks(axis):
    size, out = lax.axis_size(axis), []
    while size > 1:
        size //= 2
        out.append((axis, size))
    return out


def partner(block, bit):
    axis, mask = bit
    return lax.ppermute(block, axis, [(i, i ^ mask) for i in range(lax.axis_size(axis))])


def inner_rows(bit, done, order, unit):
    for other in done:
        if order.index(other) > order.index(bit):
            unit *= 2
    return unit


def join(a, b, inner):
    pair = [part.reshape(-1, inner, part.shape[-1]) for part in (a, b)]
    return jnp.concatenate(pair, axis=1).reshape(-1, a.shape[-1])


def halves(block, inner):
    split = block.reshape(-1, 2, inner, block.shape[1])
    return [split[:, i].reshape(-1, block.shape[1]) for i in (0, 1)]


def is_set(bit):
    return (lax.axis_index(bit[0]) & bit[1]) > 0


def add(a, b):
    return (a.astype(F32) + b.astype(F32)).astype(BF16)


def on_device(tokens, cotangent, gates, expert_ids, swap_flag, w_in, w_down):
    experts = lax.axis_size("expert")
    half_axis = experts // 2
    tok_dev, dim = tokens.shape
    units = w_down.shape[1]

    across, within = masks("dp"), masks("expert")
    core, near, far = within[-1], within[-2:-1], within[:-2]
    first = near + across
    second = across + near
    order = first[::-1] + far[::-1]
    rows_all = tok_dev * lax.axis_size("dp") * experts
    top = far[0]

    slots = jnp.arange(experts, dtype=jnp.int32)
    dense = jnp.sum(
        jnp.where(expert_ids[:, :, None] == slots, gates[:, :, None], 0.0), axis=1
    )
    parts = jnp.concatenate(split_three(dense), axis=1)
    width = rounded_up(parts.shape[1], 128)
    parts = jnp.pad(parts, ((0, 0), (0, width - parts.shape[1])))
    payload = jnp.stack([jnp.concatenate([rows, parts], axis=1) for rows in (tokens, cotangent)])

    def far_gather(block, seen):
        for i in range(0, len(far), 2):
            group = far[i : i + 2]
            flat = block.reshape(-1, block.shape[2])

            def arrived(mask):
                return partner(flat, ("expert", mask)).reshape(block.shape)

            a = group[0]
            if len(group) == 2:
                b = group[1]
                fours = [block, arrived(b[1]), arrived(a[1]), arrived(a[1] | b[1])]
                seen.append(fours[1])
                pairs = [jnp.concatenate(fours[:2], axis=1), jnp.concatenate(fours[2:], axis=1)]
            else:
                pairs = [block, arrived(a[1])]
                seen.append(pairs[1])
            if a == top:
                turn = is_set(top)
                pairs = [jnp.where(turn, pairs[1 - j], pairs[j]) for j in (0, 1)]
            block = jnp.concatenate(pairs, axis=1)
        return block

    def plane(rows, route):
        far_rows = rows.shape[0]
        for k, bit in enumerate(route):
            rows = join(rows, partner(rows, bit), inner_rows(bit, route[:k], order, far_rows))
        return rows

    def stage(after, weight, name):
        return pl.pallas_call(
            stage_kernel,
            out_shape=jax.ShapeDtypeStruct(weight.shape, BF16),
            in_specs=[ANY] * 2,
            out_specs=VMEM,
            scratch_shapes=[pltpu.SemaphoreType.DMA((CHUNKS,))],
            compiler_params=params(STAGE_MIB),
            cost_estimate=cost(0, 4 * weight.size),
            name=name,
        )(after, weight)

    seen = []
    x_far, y_far = far_gather(payload, seen)
    win = stage(seen[0], w_in.reshape(2 * units, dim), "stage_in")
    wdown = stage(seen[0], w_down.reshape(units, dim), "stage_down")
    xa, ya = plane(x_far, first), plane(y_far, second)
    xb, yb = partner(xa, core), partner(ya, core)

    half_rows = rows_all // 2
    limit = 60 if rows_all > 512 else 24
    rows_out = [jax.ShapeDtypeStruct((half_rows, dim), BF16)] * 2
    gate_type = jax.ShapeDtypeStruct((rows_all, 128), F32)
    saved_type = jax.ShapeDtypeStruct((units, rows_all), F32)
    product = 2 * rows_all * units * dim
    act, silu, slope = pl.pallas_call(
        hidden_kernel,
        out_shape=[
            jax.ShapeDtypeStruct((units, rows_all), BF16),
            saved_type,
            saved_type,
        ],
        in_specs=[ANY, ANY, VMEM, ANY],
        out_specs=[VMEM] * 3,
        scratch_shapes=[
            pltpu.VMEM((rows_all, dim), BF16),
            pltpu.VMEM((2 * units, rows_all), F32),
            pltpu.SemaphoreType.DMA((2 * CHUNKS,)),
        ],
        compiler_params=params(limit),
        cost_estimate=cost(2 * product, 4 * dim * (units + rows_all)),
        name="hidden",
    )(xa, xb, win, wdown)
    factors, gate, gate_held = pl.pallas_call(
        functools.partial(factor_kernel, experts),
        out_shape=[jax.ShapeDtypeStruct((3 * units, rows_all), BF16), gate_type, gate_type],
        in_specs=[SMEM] + [ANY] * 4 + [VMEM] * 4,
        out_specs=[VMEM] * 3,
        scratch_shapes=[
            pltpu.VMEM((rows_all, dim), BF16),
            pltpu.VMEM((units, rows_all), F32),
            pltpu.VMEM((rows_all, width), BF16),
            pltpu.SemaphoreType.DMA((2 + 2 * CHUNKS,)),
        ],
        compiler_params=params(limit),
        cost_estimate=cost(product, 2 * dim * (units + rows_all)),
        name="factors",
    )(swap_flag, xa, xb, ya, yb, act, silu, slope, wdown)
    far_factors = partner(factors, ("expert", half_axis))
    mixed_keep, back_keep, send = pl.pallas_call(
        output_kernel,
        out_shape=[
            jax.ShapeDtypeStruct((half_rows, dim), BF16),
            jax.ShapeDtypeStruct((half_rows, dim), BF16),
            jax.ShapeDtypeStruct((half_rows, 2 * dim), BF16),
        ],
        in_specs=[VMEM] * 4,
        out_specs=[VMEM] * 3,
        scratch_shapes=[
            pltpu.VMEM((rows_all, units), BF16),
            pltpu.VMEM((rows_all, 2 * units), BF16),
        ],
        compiler_params=params(limit),
        cost_estimate=cost(3 * product, 6 * dim * (units + rows_all)),
        name="outputs",
    )(gate, factors, win, wdown)

    def added(keep, got, bit, left):
        inner = inner_rows(bit, left, order, tok_dev)
        return [add(*pair) for pair in zip(halves(keep, inner), halves(got, inner))]

    def far_sends(keep, groups):
        group = groups[-1]
        a = group[0]
        inner = keep.shape[0] // 2
        pair = [keep[:inner], keep[inner:]]
        if a == top:
            turn = is_set(top)
            pair = [jnp.where(turn, pair[1 - j], pair[j]) for j in (0, 1)]
        if len(group) == 1:
            return pair[0], [(pair[1], a[1])]
        b = group[1]
        low = inner // 2
        return pair[0][:low], [
            (pair[0][low:], b[1]),
            (pair[1][:low], a[1]),
            (pair[1][low:], a[1] | b[1]),
        ]

    def far_sum(mine, sends):
        arrived = [partner(rows, ("expert", mask)) for rows, mask in sends]
        total = mine.astype(F32)
        for rows in arrived:
            total = total + rows.astype(F32)
        return total.astype(BF16), arrived[0]

    groups = [far[i : i + 2] for i in range(0, len(far), 2)]

    def plane_step(keep, got, route, k):
        left = set(order) - set(route[: k + 1])
        keep, sent = added(keep, got, route[k], left)
        return keep, partner(sent, route[k]), sent

    def zero_after(*arrays):
        return pl.pallas_call(
            zero_kernel,
            out_shape=jax.ShapeDtypeStruct((16, dim), BF16),
            in_specs=[ANY] * len(arrays),
            out_specs=VMEM,
            compiler_params=params(2),
            name="zero",
        )(*arrays)[:1]

    def weight_gradient(after, first, groups, pieces, scaled, name):
        return pl.pallas_call(
            functools.partial(weight_kernel, first, scaled),
            out_shape=jax.ShapeDtypeStruct((groups, units, dim), BF16),
            in_specs=[SMEM] + [VMEM] * 3 + [ANY] * (2 + len(after)),
            out_specs=ANY,
            scratch_shapes=[
                pltpu.VMEM((rows_all, dim), BF16),
                pltpu.VMEM((groups * units, rows_all), BF16),
                pltpu.VMEM((groups * units, dim), BF16),
                pltpu.SemaphoreType.DMA(((2 + groups) * CHUNKS,)),
            ],
            compiler_params=params(limit),
            cost_estimate=cost(groups * product, 2 * dim * (groups * units + rows_all)),
            name=name,
        )(swap_flag, factors, far_factors, gate_held, *pieces, *after)

    across_first, near_first = first[::-1], second[::-1]
    got = partner(send, core)
    mixed_keep, mixed_got, mixed_sent = plane_step(mixed_keep, got[:, :dim], across_first, 0)
    back_keep, back_got, back_sent = plane_step(back_keep, got[:, dim:], near_first, 0)
    for k in range(1, len(first)):
        mixed_keep, mixed_got, mixed_sent = plane_step(mixed_keep, mixed_got, across_first, k)
        back_keep, back_got, back_sent = plane_step(back_keep, back_got, near_first, k)
    zero = zero_after(far_factors, mixed_sent, back_sent)
    both = jnp.concatenate(
        [add(mixed_keep, mixed_got + zero), add(back_keep, back_got + zero)], axis=1
    )
    for group in groups[::-1]:
        mine, sends = far_sends(both, [group])
        both, _ = far_sum(mine, sends)
    mixed, grad_tokens = both[:, :dim], both[:, dim:]
    behind = [rows for rows, _ in sends]
    new_down = weight_gradient(behind, 0, 1, (ya, yb), True, "grad_down")
    new_in = weight_gradient(behind, 1, 2, (xa, xb), False, "grad_in")
    return (mixed, grad_tokens, new_in.reshape(w_in.shape), new_down.reshape(w_down.shape))


def solution(mesh):
    rows = P(("dp", "expert"), None)
    w_in, w_down = P("expert", None, "dp", None), P("expert", "dp", None)
    return jax.shard_map(
        on_device,
        mesh=mesh,
        in_specs=(rows, rows, rows, rows, P(), w_in, w_down),
        out_specs=(rows, rows, w_in, w_down),
        check_vma=False,
    )
```

```python
import functools

import jax
import jax.numpy as jnp
from jax import lax
from jax.experimental import pallas as pl
from jax.experimental.pallas import tpu as pltpu
from jax.sharding import PartitionSpec as P

F32, BF16 = jnp.float32, jnp.bfloat16
ANY = pl.BlockSpec(memory_space=pl.ANY)
SMEM = pl.BlockSpec(memory_space=pltpu.SMEM)
VMEM = pl.BlockSpec(memory_space=pltpu.VMEM)
CHUNKS = 4
ROW_BLOCK = 256
STAGE_MIB = 40


def nt(a, b):
    return lax.dot_general(a, b, (((1,), (1,)), ((), ())), preferred_element_type=F32)


def nn(a, b):
    return jnp.dot(a, b, preferred_element_type=F32)


def each_rows(total, body):
    if total <= ROW_BLOCK:
        body(pl.ds(0, total))
    else:

        @pl.loop(0, total // ROW_BLOCK)
        def _(i):
            body(pl.ds(pl.multiple_of(i * ROW_BLOCK, ROW_BLOCK), ROW_BLOCK))


def columns(dim):
    step = dim // CHUNKS
    return [pl.ds(c * step, step) for c in range(CHUNKS)]


def started(sems, base, pairs):
    copies = [
        pltpu.make_async_copy(source, target, sems.at[base + i])
        for i, (source, target) in enumerate(pairs)
    ]
    for copy in copies:
        copy.start()
    return copies


def wait(copies):
    for copy in copies:
        copy.wait()


def row_copies(own, received, buffer, cols, target=None):
    half = own.shape[0]
    target = cols if target is None else target
    return [
        (own.at[:, cols], buffer.at[pl.ds(0, half), target]),
        (received.at[:, cols], buffer.at[pl.ds(half, half), target]),
    ]


def split_three(x):
    high = x.astype(BF16)
    rest = x - high.astype(F32)
    middle = rest.astype(BF16)
    low = (rest - middle.astype(F32)).astype(BF16)
    return high, middle, low


def gate_column(parts, expert, experts):
    lane = lax.broadcasted_iota(jnp.int32, parts.shape, 1)
    values = parts.astype(F32)
    high, middle, low = (
        jnp.sum(jnp.where(lane == expert + i * experts, values, 0.0), axis=1, keepdims=True)
        for i in range(3)
    )
    return (low + middle) + high


def fill_gates(parts, gate, expert, experts):
    def body(rows):
        column = gate_column(parts[rows, :], expert, experts)
        gate[rows, :] = jnp.broadcast_to(column, (column.shape[0], gate.shape[1]))

    each_rows(parts.shape[0], body)


def held_expert(flags):
    me = lax.axis_index("expert")
    flag = flags[me]
    return me, jnp.where(flag > 0, me ^ (lax.axis_size("expert") // 2), me), flag


def stage_kernel(*refs):
    weight, out, sems = refs[-3:]
    wait(started(sems, 0, [(weight.at[:, c], out.at[:, c]) for c in columns(weight.shape[1])]))


def zero_kernel(*refs):
    refs[-1][...] = jnp.zeros_like(refs[-1])


def hidden_kernel(xa, xb, win, after, act, silu, slope, x, hidden, sems):
    units, rows_all = act.shape
    dim = win.shape[1]
    loads = []
    for c, cols in enumerate(columns(dim)):
        loads.append(started(sems, 2 * c, row_copies(xa, xb, x, cols)))
    for c, cols in enumerate(columns(dim)):
        wait(loads[c])

        def multiply(rows):
            product = nt(win[:, cols], x[rows, cols])
            hidden[:, rows] = product if c == 0 else hidden[:, rows] + product

        each_rows(rows_all, multiply)

    def pointwise(rows):
        g, u = hidden[pl.ds(0, units), rows], hidden[pl.ds(units, units), rows]
        sig = jax.nn.sigmoid(g)
        gated = g * sig
        silu[:, rows] = gated
        slope[:, rows] = u * sig * (1.0 + g * (1.0 - sig))
        act[:, rows] = (gated * u).astype(BF16)

    each_rows(rows_all, pointwise)


def split_product(rows_ref, weight, keep, send, finish):
    half, dim = send.shape
    for cols in columns(dim):

        def multiply(start, target):
            def body(rows):
                mine = pl.ds(rows.start + start, rows.size)
                product = nn(rows_ref[mine, :], weight[:, cols]).astype(BF16)
                target[rows, cols] = finish(mine, product)

            return body

        each_rows(half, multiply(half, send))
        each_rows(half, multiply(0, keep))


def part_kernel(
    experts, flags, xa, xb, act, wdown, keep, send, gate, gate_held, parts, rows_act, sems
):
    dim = wdown.shape[1]
    rows_all, width = parts.shape
    loads = started(sems, 0, row_copies(xa, xb, parts, pl.ds(dim, width), pl.ds(0, width)))

    def turn(rows):
        rows_act[rows, :] = act[:, rows].T

    each_rows(rows_all, turn)
    me, held, _ = held_expert(flags)
    wait(loads)
    fill_gates(parts, gate, me, experts)
    fill_gates(parts, gate_held, held, experts)

    def weighted(rows, part):
        return (gate[rows, pl.ds(0, 1)] * part.astype(F32)).astype(BF16)

    split_product(rows_act, wdown, keep, send, weighted)


def back_kernel(factors, win, after, keep, send, rows_grad):
    units = win.shape[0] // 2

    def turn(rows):
        rows_grad[rows, :] = factors[pl.ds(units, 2 * units), rows].T

    each_rows(rows_grad.shape[0], turn)
    split_product(rows_grad, win, keep, send, lambda rows, part: part)


def factor_kernel(
    ya, yb, act, silu, slope, gate, wdown, after, factors, y, total, sems
):
    units, dim = wdown.shape
    rows_all = y.shape[0]
    loads = []
    for c, cols in enumerate(columns(dim)):
        loads.append(started(sems, 2 * c, row_copies(ya, yb, y, cols)))
    factors[pl.ds(0, units), :] = act[...]
    for c, cols in enumerate(columns(dim)):
        wait(loads[c])

        def multiply(rows):
            scaled = (gate[rows, pl.ds(0, 1)] * y[rows, cols].astype(F32)).astype(BF16)
            product = nt(wdown[:, cols], scaled)
            total[:, rows] = product if c == 0 else total[:, rows] + product

        each_rows(rows_all, multiply)

    def pointwise(rows):
        value = total[:, rows]
        factors[pl.ds(units, units), rows] = (value * slope[:, rows]).astype(BF16)
        factors[pl.ds(2 * units, units), rows] = (value * silu[:, rows]).astype(BF16)

    each_rows(rows_all, pointwise)


def weight_kernel(first, scaled, flags, own, away, gate, ra, rb, *rest):
    grads, r, used, out, sems = rest[-5:]
    groups, units, dim = grads.shape
    rows_all = r.shape[0]
    base, loads, stores = 0, [], []
    for cols in columns(dim):
        loads.append(started(sems, base, row_copies(ra, rb, r, cols)))
        base += 2
    _, _, flag = held_expert(flags)
    some = pl.ds(first * units, groups * units)
    used[...] = jnp.where(flag > 0, away[some, :], own[some, :])
    for c, cols in enumerate(columns(dim)):
        wait(loads[c])
        if scaled:

            def scale(rows):
                r[rows, cols] = (gate[rows, pl.ds(0, 1)] * r[rows, cols].astype(F32)).astype(BF16)

            each_rows(rows_all, scale)
        pairs = []
        for i in range(groups):
            some = pl.ds(i * units, units)
            out[some, cols] = nn(used[some, :], r[:, cols]).astype(BF16)
            pairs.append((out.at[some, cols], grads.at[i, :, cols]))
        stores.append(started(sems, base, pairs))
        base += groups
    for store in stores:
        wait(store)


def rounded_up(value, unit):
    return -(-value // unit) * unit


def params(mib):
    return pltpu.CompilerParams(vmem_limit_bytes=mib * 1024 * 1024)


def cost(flops, size):
    return pl.CostEstimate(flops=flops, bytes_accessed=size, transcendentals=0)


def masks(axis):
    size, out = lax.axis_size(axis), []
    while size > 1:
        size //= 2
        out.append((axis, size))
    return out


def partner(block, bit):
    axis, mask = bit
    return lax.ppermute(block, axis, [(i, i ^ mask) for i in range(lax.axis_size(axis))])


def inner_rows(bit, done, order, unit):
    for other in done:
        if order.index(other) > order.index(bit):
            unit *= 2
    return unit


def join(a, b, inner):
    pair = [part.reshape(-1, inner, part.shape[-1]) for part in (a, b)]
    return jnp.concatenate(pair, axis=1).reshape(-1, a.shape[-1])


def halves(block, inner):
    split = block.reshape(-1, 2, inner, block.shape[1])
    return [split[:, i].reshape(-1, block.shape[1]) for i in (0, 1)]


def is_set(bit):
    return (lax.axis_index(bit[0]) & bit[1]) > 0


def add(a, b):
    return (a.astype(F32) + b.astype(F32)).astype(BF16)


def on_device(tokens, cotangent, gates, expert_ids, swap_flag, w_in, w_down):
    experts = lax.axis_size("expert")
    half_axis = experts // 2
    tok_dev, dim = tokens.shape
    units = w_down.shape[1]

    across, within = masks("dp"), masks("expert")
    core, near, far = within[-1], within[-2:-1], within[:-2]
    first = near + across
    second = across + near
    order = first[::-1] + far[::-1]
    rows_all = tok_dev * lax.axis_size("dp") * experts
    top = far[0]

    slots = jnp.arange(experts, dtype=jnp.int32)
    dense = jnp.sum(
        jnp.where(expert_ids[:, :, None] == slots, gates[:, :, None], 0.0), axis=1
    )
    parts = jnp.concatenate(split_three(dense), axis=1)
    width = rounded_up(parts.shape[1], 128)
    parts = jnp.pad(parts, ((0, 0), (0, width - parts.shape[1])))
    payload = jnp.stack([jnp.concatenate([rows, parts], axis=1) for rows in (tokens, cotangent)])

    def far_gather(block, seen):
        for i in range(0, len(far), 2):
            group = far[i : i + 2]
            flat = block.reshape(-1, block.shape[2])

            def arrived(mask):
                return partner(flat, ("expert", mask)).reshape(block.shape)

            a = group[0]
            if len(group) == 2:
                b = group[1]
                fours = [block, arrived(b[1]), arrived(a[1]), arrived(a[1] | b[1])]
                seen.append(fours[1])
                pairs = [jnp.concatenate(fours[:2], axis=1), jnp.concatenate(fours[2:], axis=1)]
            else:
                pairs = [block, arrived(a[1])]
                seen.append(pairs[1])
            if a == top:
                turn = is_set(top)
                pairs = [jnp.where(turn, pairs[1 - j], pairs[j]) for j in (0, 1)]
            block = jnp.concatenate(pairs, axis=1)
        return block

    def plane_step_out(rows, route, k, zero=None):
        got = partner(rows, route[k])
        got = got if zero is None else got + zero
        return join(rows, got, inner_rows(route[k], route[:k], order, far_rows))

    def zero_after(columns_of, *arrays):
        return pl.pallas_call(
            zero_kernel,
            out_shape=jax.ShapeDtypeStruct((16, columns_of), BF16),
            in_specs=[ANY] * len(arrays),
            out_specs=VMEM,
            compiler_params=params(2),
            name="zero",
        )(*arrays)[:1]

    def stage(weight, after, name):
        return pl.pallas_call(
            stage_kernel,
            out_shape=jax.ShapeDtypeStruct(weight.shape, BF16),
            in_specs=[ANY] * (len(after) + 1),
            out_specs=VMEM,
            scratch_shapes=[pltpu.SemaphoreType.DMA((CHUNKS,))],
            compiler_params=params(STAGE_MIB),
            cost_estimate=cost(0, 4 * weight.size),
            name=name,
        )(*after, weight)

    seen = []
    x_far, y_far = far_gather(payload, seen)
    far_rows = x_far.shape[0]
    xa, ya = x_far, y_far
    for k in range(len(first)):
        zero = None
        if k == len(first) - 1:
            win = stage(w_in.reshape(2 * units, dim), (xa, ya), "stage_in")
            wdown = stage(w_down.reshape(units, dim), (xa, ya), "stage_down")
            zero = zero_after(dim + width, win, wdown)
        xa, ya = plane_step_out(xa, first, k, zero), plane_step_out(ya, second, k)
    xb, yb = partner(xa, core), partner(ya, core)

    half_rows = rows_all // 2
    limit = 60 if rows_all > 512 else 24
    row_type = jax.ShapeDtypeStruct((half_rows, dim), BF16)
    gate_type = jax.ShapeDtypeStruct((rows_all, 128), F32)
    saved_type = jax.ShapeDtypeStruct((units, rows_all), F32)
    product = 2 * rows_all * units * dim
    act, silu, slope = pl.pallas_call(
        hidden_kernel,
        out_shape=[
            jax.ShapeDtypeStruct((units, rows_all), BF16),
            saved_type,
            saved_type,
        ],
        in_specs=[ANY, ANY, VMEM, ANY],
        out_specs=[VMEM] * 3,
        scratch_shapes=[
            pltpu.VMEM((rows_all, dim), BF16),
            pltpu.VMEM((2 * units, rows_all), F32),
            pltpu.SemaphoreType.DMA((2 * CHUNKS,)),
        ],
        compiler_params=params(limit),
        cost_estimate=cost(2 * product, 4 * dim * (units + rows_all)),
        name="hidden",
    )(xa, xb, win, wdown)
    mixed_keep, mixed_send, gate, gate_held = pl.pallas_call(
        functools.partial(part_kernel, experts),
        out_shape=[row_type, row_type, gate_type, gate_type],
        in_specs=[SMEM, ANY, ANY, VMEM, VMEM],
        out_specs=[VMEM] * 4,
        scratch_shapes=[
            pltpu.VMEM((rows_all, width), BF16),
            pltpu.VMEM((rows_all, units), BF16),
            pltpu.SemaphoreType.DMA((2,)),
        ],
        compiler_params=params(limit),
        cost_estimate=cost(product, 2 * dim * (units + rows_all)),
        name="part",
    )(swap_flag, xa, xb, act, wdown)
    factors = pl.pallas_call(
        factor_kernel,
        out_shape=jax.ShapeDtypeStruct((3 * units, rows_all), BF16),
        in_specs=[ANY] * 2 + [VMEM] * 5 + [ANY],
        out_specs=VMEM,
        scratch_shapes=[
            pltpu.VMEM((rows_all, dim), BF16),
            pltpu.VMEM((units, rows_all), F32),
            pltpu.SemaphoreType.DMA((2 * CHUNKS,)),
        ],
        compiler_params=params(limit),
        cost_estimate=cost(product, 2 * dim * (units + rows_all)),
        name="factors",
    )(ya, yb, act, silu, slope, gate, wdown, mixed_send)
    far_factors = partner(factors, ("expert", half_axis))
    mixed_got = partner(mixed_send, core)
    back_keep, back_send = pl.pallas_call(
        back_kernel,
        out_shape=[row_type, row_type],
        in_specs=[VMEM] * 2 + [ANY],
        out_specs=[VMEM] * 2,
        scratch_shapes=[pltpu.VMEM((rows_all, 2 * units), BF16)],
        compiler_params=params(limit),
        cost_estimate=cost(2 * product, 4 * dim * (units + rows_all)),
        name="back",
    )(factors, win, mixed_got)

    def added(keep, got, bit, left):
        inner = inner_rows(bit, left, order, tok_dev)
        return [add(*pair) for pair in zip(halves(keep, inner), halves(got, inner))]

    def far_step(keep, bit):
        inner = far_inner[bit]
        pair = halves(keep, inner)
        if bit == top:
            turn = is_set(top)
            pair = [jnp.where(turn, pair[1 - j], pair[j]) for j in (0, 1)]
        got = partner(pair[1], bit)
        return add(pair[0], got), pair[1]

    groups = [far[i : i + 2] for i in range(0, len(far), 2)]
    layout = [bit for group in groups[::-1] for bit in group]
    far_inner, left = {}, list(layout)
    for bit in far[::-1]:
        place = left.index(bit)
        far_inner[bit] = tok_dev * 2 ** (len(left) - 1 - place)
        left.remove(bit)

    def plane_step(keep, got, route, k):
        left = set(order) - set(route[: k + 1])
        keep, sent = added(keep, got, route[k], left)
        return keep, partner(sent, route[k]), sent

    def weight_gradient(after, first, groups, pieces, scaled, name):
        return pl.pallas_call(
            functools.partial(weight_kernel, first, scaled),
            out_shape=jax.ShapeDtypeStruct((groups, units, dim), BF16),
            in_specs=[SMEM] + [VMEM] * 3 + [ANY] * (2 + len(after)),
            out_specs=ANY,
            scratch_shapes=[
                pltpu.VMEM((rows_all, dim), BF16),
                pltpu.VMEM((groups * units, rows_all), BF16),
                pltpu.VMEM((groups * units, dim), BF16),
                pltpu.SemaphoreType.DMA(((2 + groups) * CHUNKS,)),
            ],
            compiler_params=params(limit),
            cost_estimate=cost(groups * product, 2 * dim * (groups * units + rows_all)),
            name=name,
        )(swap_flag, factors, far_factors, gate_held, *pieces, *after)

    across_first, near_first = first[::-1], second[::-1]
    back_got = partner(back_send, core)
    for k in range(len(first)):
        if k > 0:
            mixed_got = mixed_got + zero_after(dim, back_sent)
        mixed_keep, mixed_got, mixed_sent = plane_step(mixed_keep, mixed_got, across_first, k)
        back_keep, back_got, back_sent = plane_step(back_keep, back_got, near_first, k)
    both = jnp.concatenate([add(mixed_keep, mixed_got), add(back_keep, back_got)], axis=1)
    for bit in far[:0:-1]:
        both, sent = far_step(both, bit)
    both, sent = far_step(both + zero_after(2 * dim, far_factors, sent), far[0])
    mixed, grad_tokens = both[:, :dim], both[:, dim:]
    behind = [sent]
    new_down = weight_gradient(behind, 0, 1, (ya, yb), True, "grad_down")
    new_in = weight_gradient(behind, 1, 2, (xa, xb), False, "grad_in")
    return (mixed, grad_tokens, new_in.reshape(w_in.shape), new_down.reshape(w_down.shape))


def solution(mesh):
    rows = P(("dp", "expert"), None)
    w_in, w_down = P("expert", None, "dp", None), P("expert", "dp", None)
    return jax.shard_map(
        on_device,
        mesh=mesh,
        in_specs=(rows, rows, rows, rows, P(), w_in, w_down),
        out_specs=(rows, rows, w_in, w_down),
        check_vma=False,
    )
```

```python
import functools

import jax
import jax.numpy as jnp
from jax import lax
from jax.experimental import pallas as pl
from jax.experimental.pallas import tpu as pltpu
from jax.sharding import PartitionSpec as P

F32, BF16 = jnp.float32, jnp.bfloat16
ANY = pl.BlockSpec(memory_space=pl.ANY)
SMEM = pl.BlockSpec(memory_space=pltpu.SMEM)
VMEM = pl.BlockSpec(memory_space=pltpu.VMEM)
CHUNKS = 4
ROW_BLOCK = 256
STAGE_MIB = 40


def nt(a, b):
    return lax.dot_general(a, b, (((1,), (1,)), ((), ())), preferred_element_type=F32)


def nn(a, b):
    return jnp.dot(a, b, preferred_element_type=F32)


def each_rows(total, body):
    if total <= ROW_BLOCK:
        body(pl.ds(0, total))
    else:

        @pl.loop(0, total // ROW_BLOCK)
        def _(i):
            body(pl.ds(pl.multiple_of(i * ROW_BLOCK, ROW_BLOCK), ROW_BLOCK))


def columns(dim):
    step = dim // CHUNKS
    return [pl.ds(c * step, step) for c in range(CHUNKS)]


def started(sems, base, pairs):
    copies = [
        pltpu.make_async_copy(source, target, sems.at[base + i])
        for i, (source, target) in enumerate(pairs)
    ]
    for copy in copies:
        copy.start()
    return copies


def wait(copies):
    for copy in copies:
        copy.wait()


def row_copies(own, received, buffer, cols, target=None):
    half = own.shape[0]
    target = cols if target is None else target
    return [
        (own.at[:, cols], buffer.at[pl.ds(0, half), target]),
        (received.at[:, cols], buffer.at[pl.ds(half, half), target]),
    ]


def split_three(x):
    high = x.astype(BF16)
    rest = x - high.astype(F32)
    middle = rest.astype(BF16)
    low = (rest - middle.astype(F32)).astype(BF16)
    return high, middle, low


def gate_column(parts, expert, experts):
    lane = lax.broadcasted_iota(jnp.int32, parts.shape, 1)
    values = parts.astype(F32)
    high, middle, low = (
        jnp.sum(jnp.where(lane == expert + i * experts, values, 0.0), axis=1, keepdims=True)
        for i in range(3)
    )
    return (low + middle) + high


def fill_gates(parts, gate, expert, experts):
    def body(rows):
        column = gate_column(parts[rows, :], expert, experts)
        gate[rows, :] = jnp.broadcast_to(column, (column.shape[0], gate.shape[1]))

    each_rows(parts.shape[0], body)


def held_expert(flags):
    me = lax.axis_index("expert")
    flag = flags[me]
    return me, jnp.where(flag > 0, me ^ (lax.axis_size("expert") // 2), me), flag


def stage_kernel(*refs):
    weight, out, sems = refs[-3:]
    wait(started(sems, 0, [(weight.at[:, c], out.at[:, c]) for c in columns(weight.shape[1])]))


def zero_kernel(*refs):
    refs[-1][...] = jnp.zeros_like(refs[-1])


def hidden_kernel(xa, xb, win, after, act, silu, slope, x, hidden, sems):
    units, rows_all = act.shape
    dim = win.shape[1]
    loads = []
    for c, cols in enumerate(columns(dim)):
        loads.append(started(sems, 2 * c, row_copies(xa, xb, x, cols)))
    for c, cols in enumerate(columns(dim)):
        wait(loads[c])

        def multiply(rows):
            product = nt(win[:, cols], x[rows, cols])
            hidden[:, rows] = product if c == 0 else hidden[:, rows] + product

        each_rows(rows_all, multiply)

    def pointwise(rows):
        g, u = hidden[pl.ds(0, units), rows], hidden[pl.ds(units, units), rows]
        sig = jax.nn.sigmoid(g)
        gated = g * sig
        silu[:, rows] = gated
        slope[:, rows] = u * sig * (1.0 + g * (1.0 - sig))
        act[:, rows] = (gated * u).astype(BF16)

    each_rows(rows_all, pointwise)


def split_product(rows_ref, weight, keep, send, finish):
    half, dim = send.shape
    for cols in columns(dim):

        def multiply(start, target):
            def body(rows):
                mine = pl.ds(rows.start + start, rows.size)
                product = nn(rows_ref[mine, :], weight[:, cols]).astype(BF16)
                target[rows, cols] = finish(mine, product)

            return body

        each_rows(half, multiply(half, send))
        each_rows(half, multiply(0, keep))


def part_kernel(
    experts, flags, xa, xb, act, wdown, keep, send, gate, gate_held, parts, rows_act, sems
):
    dim = wdown.shape[1]
    rows_all, width = parts.shape
    loads = started(sems, 0, row_copies(xa, xb, parts, pl.ds(dim, width), pl.ds(0, width)))

    def turn(rows):
        rows_act[rows, :] = act[:, rows].T

    each_rows(rows_all, turn)
    me, held, _ = held_expert(flags)
    wait(loads)
    fill_gates(parts, gate, me, experts)
    fill_gates(parts, gate_held, held, experts)

    def weighted(rows, part):
        return (gate[rows, pl.ds(0, 1)] * part.astype(F32)).astype(BF16)

    split_product(rows_act, wdown, keep, send, weighted)


def back_kernel(factors, win, after, keep, send, rows_grad):
    units = win.shape[0] // 2

    def turn(rows):
        rows_grad[rows, :] = factors[pl.ds(units, 2 * units), rows].T

    each_rows(rows_grad.shape[0], turn)
    split_product(rows_grad, win, keep, send, lambda rows, part: part)


def factor_kernel(
    ya, yb, act, silu, slope, gate, wdown, after, factors, y, total, sems
):
    units, dim = wdown.shape
    rows_all = y.shape[0]
    loads = []
    for c, cols in enumerate(columns(dim)):
        loads.append(started(sems, 2 * c, row_copies(ya, yb, y, cols)))
    factors[pl.ds(0, units), :] = act[...]
    for c, cols in enumerate(columns(dim)):
        wait(loads[c])

        def multiply(rows):
            scaled = (gate[rows, pl.ds(0, 1)] * y[rows, cols].astype(F32)).astype(BF16)
            product = nt(wdown[:, cols], scaled)
            total[:, rows] = product if c == 0 else total[:, rows] + product

        each_rows(rows_all, multiply)

    def pointwise(rows):
        value = total[:, rows]
        factors[pl.ds(units, units), rows] = (value * slope[:, rows]).astype(BF16)
        factors[pl.ds(2 * units, units), rows] = (value * silu[:, rows]).astype(BF16)

    each_rows(rows_all, pointwise)


def weight_kernel(first, scaled, flags, own, away, gate, ra, rb, *rest):
    grads, r, used, out, sems = rest[-5:]
    groups, units, dim = grads.shape
    rows_all = r.shape[0]
    base, loads, stores = 0, [], []
    for cols in columns(dim):
        loads.append(started(sems, base, row_copies(ra, rb, r, cols)))
        base += 2
    _, _, flag = held_expert(flags)
    some = pl.ds(first * units, groups * units)
    used[...] = jnp.where(flag > 0, away[some, :], own[some, :])
    for c, cols in enumerate(columns(dim)):
        wait(loads[c])
        if scaled:

            def scale(rows):
                r[rows, cols] = (gate[rows, pl.ds(0, 1)] * r[rows, cols].astype(F32)).astype(BF16)

            each_rows(rows_all, scale)
        pairs = []
        for i in range(groups):
            some = pl.ds(i * units, units)
            out[some, cols] = nn(used[some, :], r[:, cols]).astype(BF16)
            pairs.append((out.at[some, cols], grads.at[i, :, cols]))
        stores.append(started(sems, base, pairs))
        base += groups
    for store in stores:
        wait(store)


def rounded_up(value, unit):
    return -(-value // unit) * unit


def params(mib):
    return pltpu.CompilerParams(vmem_limit_bytes=mib * 1024 * 1024)


def cost(flops, size):
    return pl.CostEstimate(flops=flops, bytes_accessed=size, transcendentals=0)


def masks(axis):
    size, out = lax.axis_size(axis), []
    while size > 1:
        size //= 2
        out.append((axis, size))
    return out


def partner(block, bit):
    axis, mask = bit
    return lax.ppermute(block, axis, [(i, i ^ mask) for i in range(lax.axis_size(axis))])


def inner_rows(bit, done, order, unit):
    for other in done:
        if order.index(other) > order.index(bit):
            unit *= 2
    return unit


def join(a, b, inner):
    pair = [part.reshape(-1, inner, part.shape[-1]) for part in (a, b)]
    return jnp.concatenate(pair, axis=1).reshape(-1, a.shape[-1])


def halves(block, inner):
    split = block.reshape(-1, 2, inner, block.shape[1])
    return [split[:, i].reshape(-1, block.shape[1]) for i in (0, 1)]


def is_set(bit):
    return (lax.axis_index(bit[0]) & bit[1]) > 0


def add(a, b):
    return (a.astype(F32) + b.astype(F32)).astype(BF16)


def on_device(tokens, cotangent, gates, expert_ids, swap_flag, w_in, w_down):
    experts = lax.axis_size("expert")
    half_axis = experts // 2
    tok_dev, dim = tokens.shape
    units = w_down.shape[1]

    across, within = masks("dp"), masks("expert")
    core, near, far = within[-1], within[-2:-1], within[:-2]
    first = near + across
    second = across + near
    order = first[::-1] + far[::-1]
    rows_all = tok_dev * lax.axis_size("dp") * experts
    top = far[0]

    slots = jnp.arange(experts, dtype=jnp.int32)
    dense = jnp.sum(
        jnp.where(expert_ids[:, :, None] == slots, gates[:, :, None], 0.0), axis=1
    )
    parts = jnp.concatenate(split_three(dense), axis=1)
    width = rounded_up(parts.shape[1], 128)
    parts = jnp.pad(parts, ((0, 0), (0, width - parts.shape[1])))
    payload = jnp.stack([jnp.concatenate([rows, parts], axis=1) for rows in (tokens, cotangent)])

    def far_gather(block, seen):
        for i in range(0, len(far), 2):
            group = far[i : i + 2]
            flat = block.reshape(-1, block.shape[2])

            def arrived(mask):
                return partner(flat, ("expert", mask)).reshape(block.shape)

            a = group[0]
            if len(group) == 2:
                b = group[1]
                fours = [block, arrived(b[1]), arrived(a[1]), arrived(a[1] | b[1])]
                seen.append(fours[1])
                pairs = [jnp.concatenate(fours[:2], axis=1), jnp.concatenate(fours[2:], axis=1)]
            else:
                pairs = [block, arrived(a[1])]
                seen.append(pairs[1])
            if a == top:
                turn = is_set(top)
                pairs = [jnp.where(turn, pairs[1 - j], pairs[j]) for j in (0, 1)]
            block = jnp.concatenate(pairs, axis=1)
        return block

    def plane_step_out(rows, route, k, zero=None):
        got = partner(rows, route[k])
        got = got if zero is None else got + zero
        return join(rows, got, inner_rows(route[k], route[:k], order, far_rows))

    def zero_after(columns_of, *arrays):
        return pl.pallas_call(
            zero_kernel,
            out_shape=jax.ShapeDtypeStruct((16, columns_of), BF16),
            in_specs=[ANY] * len(arrays),
            out_specs=VMEM,
            compiler_params=params(2),
            name="zero",
        )(*arrays)[:1]

    def stage(weight, after, name):
        return pl.pallas_call(
            stage_kernel,
            out_shape=jax.ShapeDtypeStruct(weight.shape, BF16),
            in_specs=[ANY] * (len(after) + 1),
            out_specs=VMEM,
            scratch_shapes=[pltpu.SemaphoreType.DMA((CHUNKS,))],
            compiler_params=params(STAGE_MIB),
            cost_estimate=cost(0, 4 * weight.size),
            name=name,
        )(*after, weight)

    seen = []
    x_far, y_far = far_gather(payload, seen)
    far_rows = x_far.shape[0]
    xa, ya = x_far, y_far
    for k in range(len(first)):
        zero = None
        if k == len(first) - 1:
            win = stage(w_in.reshape(2 * units, dim), (xa, ya), "stage_in")
            wdown = stage(w_down.reshape(units, dim), (xa, ya), "stage_down")
            zero = zero_after(dim + width, win, wdown)
        xa, ya = plane_step_out(xa, first, k, zero), plane_step_out(ya, second, k)
    xb, yb = partner(xa, core), partner(ya, core)

    half_rows = rows_all // 2
    limit = 60 if rows_all > 512 else 24
    row_type = jax.ShapeDtypeStruct((half_rows, dim), BF16)
    gate_type = jax.ShapeDtypeStruct((rows_all, 128), F32)
    saved_type = jax.ShapeDtypeStruct((units, rows_all), F32)
    product = 2 * rows_all * units * dim
    act, silu, slope = pl.pallas_call(
        hidden_kernel,
        out_shape=[
            jax.ShapeDtypeStruct((units, rows_all), BF16),
            saved_type,
            saved_type,
        ],
        in_specs=[ANY, ANY, VMEM, ANY],
        out_specs=[VMEM] * 3,
        scratch_shapes=[
            pltpu.VMEM((rows_all, dim), BF16),
            pltpu.VMEM((2 * units, rows_all), F32),
            pltpu.SemaphoreType.DMA((2 * CHUNKS,)),
        ],
        compiler_params=params(limit),
        cost_estimate=cost(2 * product, 4 * dim * (units + rows_all)),
        name="hidden",
    )(xa, xb, win, wdown)
    mixed_keep, mixed_send, gate, gate_held = pl.pallas_call(
        functools.partial(part_kernel, experts),
        out_shape=[row_type, row_type, gate_type, gate_type],
        in_specs=[SMEM, ANY, ANY, VMEM, VMEM],
        out_specs=[VMEM] * 4,
        scratch_shapes=[
            pltpu.VMEM((rows_all, width), BF16),
            pltpu.VMEM((rows_all, units), BF16),
            pltpu.SemaphoreType.DMA((2,)),
        ],
        compiler_params=params(limit),
        cost_estimate=cost(product, 2 * dim * (units + rows_all)),
        name="part",
    )(swap_flag, xa, xb, act, wdown)
    factors = pl.pallas_call(
        factor_kernel,
        out_shape=jax.ShapeDtypeStruct((3 * units, rows_all), BF16),
        in_specs=[ANY] * 2 + [VMEM] * 5 + [ANY],
        out_specs=VMEM,
        scratch_shapes=[
            pltpu.VMEM((rows_all, dim), BF16),
            pltpu.VMEM((units, rows_all), F32),
            pltpu.SemaphoreType.DMA((2 * CHUNKS,)),
        ],
        compiler_params=params(limit),
        cost_estimate=cost(product, 2 * dim * (units + rows_all)),
        name="factors",
    )(ya, yb, act, silu, slope, gate, wdown, mixed_send)
    far_factors = partner(factors, ("expert", half_axis))
    mixed_got = partner(mixed_send, core)
    back_keep, back_send = pl.pallas_call(
        back_kernel,
        out_shape=[row_type, row_type],
        in_specs=[VMEM] * 2 + [ANY],
        out_specs=[VMEM] * 2,
        scratch_shapes=[pltpu.VMEM((rows_all, 2 * units), BF16)],
        compiler_params=params(limit),
        cost_estimate=cost(2 * product, 4 * dim * (units + rows_all)),
        name="back",
    )(factors, win, mixed_got)

    def added(keep, got, bit, left):
        inner = inner_rows(bit, left, order, tok_dev)
        return [add(*pair) for pair in zip(halves(keep, inner), halves(got, inner))]

    def far_step(keep, bit):
        inner = far_inner[bit]
        pair = halves(keep, inner)
        if bit == top:
            turn = is_set(top)
            pair = [jnp.where(turn, pair[1 - j], pair[j]) for j in (0, 1)]
        got = partner(pair[1], bit)
        return add(pair[0], got), pair[1]

    groups = [far[i : i + 2] for i in range(0, len(far), 2)]
    layout = [bit for group in groups[::-1] for bit in group]
    far_inner, left = {}, list(layout)
    for bit in far[::-1]:
        place = left.index(bit)
        far_inner[bit] = tok_dev * 2 ** (len(left) - 1 - place)
        left.remove(bit)

    def plane_step(keep, got, route, k):
        left = set(order) - set(route[: k + 1])
        keep, sent = added(keep, got, route[k], left)
        return keep, partner(sent, route[k]), sent

    def weight_gradient(after, first, groups, pieces, scaled, name):
        return pl.pallas_call(
            functools.partial(weight_kernel, first, scaled),
            out_shape=jax.ShapeDtypeStruct((groups, units, dim), BF16),
            in_specs=[SMEM] + [VMEM] * 3 + [ANY] * (2 + len(after)),
            out_specs=ANY,
            scratch_shapes=[
                pltpu.VMEM((rows_all, dim), BF16),
                pltpu.VMEM((groups * units, rows_all), BF16),
                pltpu.VMEM((groups * units, dim), BF16),
                pltpu.SemaphoreType.DMA(((2 + groups) * CHUNKS,)),
            ],
            compiler_params=params(limit),
            cost_estimate=cost(groups * product, 2 * dim * (groups * units + rows_all)),
            name=name,
        )(swap_flag, factors, far_factors, gate_held, *pieces, *after)

    across_first, near_first = first[::-1], second[::-1]
    back_got = partner(back_send, core)
    for k in range(len(first)):
        if k > 0:
            mixed_got = mixed_got + zero_after(dim, back_sent)
        mixed_keep, mixed_got, mixed_sent = plane_step(mixed_keep, mixed_got, across_first, k)
        back_keep, back_got, back_sent = plane_step(back_keep, back_got, near_first, k)
    both = jnp.concatenate([add(mixed_keep, mixed_got), add(back_keep, back_got)], axis=1)
    for bit in far[:0:-1]:
        both, sent = far_step(both, bit)
    near_sent = [sent]
    both, sent = far_step(both + zero_after(2 * dim, far_factors, sent), far[0])
    mixed, grad_tokens = both[:, :dim], both[:, dim:]
    behind = [sent]
    new_down = weight_gradient(near_sent, 0, 1, (ya, yb), True, "grad_down")
    new_in = weight_gradient(behind, 1, 2, (xa, xb), False, "grad_in")
    return (mixed, grad_tokens, new_in.reshape(w_in.shape), new_down.reshape(w_down.shape))


def solution(mesh):
    rows = P(("dp", "expert"), None)
    w_in, w_down = P("expert", None, "dp", None), P("expert", "dp", None)
    return jax.shard_map(
        on_device,
        mesh=mesh,
        in_specs=(rows, rows, rows, rows, P(), w_in, w_down),
        out_specs=(rows, rows, w_in, w_down),
        check_vma=False,
    )
```

```python
import functools

import jax
import jax.numpy as jnp
from jax import lax
from jax.experimental import pallas as pl
from jax.experimental.pallas import tpu as pltpu
from jax.sharding import PartitionSpec as P

F32, BF16 = jnp.float32, jnp.bfloat16
ANY = pl.BlockSpec(memory_space=pl.ANY)
SMEM = pl.BlockSpec(memory_space=pltpu.SMEM)
VMEM = pl.BlockSpec(memory_space=pltpu.VMEM)
CHUNKS = 4
ROW_BLOCK = 256
STAGE_MIB = 40


def nt(a, b):
    return lax.dot_general(a, b, (((1,), (1,)), ((), ())), preferred_element_type=F32)


def nn(a, b):
    return jnp.dot(a, b, preferred_element_type=F32)


def each_rows(total, body):
    if total <= ROW_BLOCK:
        body(pl.ds(0, total))
    else:

        @pl.loop(0, total // ROW_BLOCK)
        def _(i):
            body(pl.ds(pl.multiple_of(i * ROW_BLOCK, ROW_BLOCK), ROW_BLOCK))


def columns(dim):
    step = dim // CHUNKS
    return [pl.ds(c * step, step) for c in range(CHUNKS)]


def started(sems, base, pairs):
    copies = [
        pltpu.make_async_copy(source, target, sems.at[base + i])
        for i, (source, target) in enumerate(pairs)
    ]
    for copy in copies:
        copy.start()
    return copies


def wait(copies):
    for copy in copies:
        copy.wait()


def row_copies(own, received, buffer, cols, target=None):
    half = own.shape[0]
    target = cols if target is None else target
    return [
        (own.at[:, cols], buffer.at[pl.ds(0, half), target]),
        (received.at[:, cols], buffer.at[pl.ds(half, half), target]),
    ]


def split_three(x):
    high = x.astype(BF16)
    rest = x - high.astype(F32)
    middle = rest.astype(BF16)
    low = (rest - middle.astype(F32)).astype(BF16)
    return high, middle, low


def gate_column(parts, expert, experts):
    lane = lax.broadcasted_iota(jnp.int32, parts.shape, 1)
    values = parts.astype(F32)
    high, middle, low = (
        jnp.sum(jnp.where(lane == expert + i * experts, values, 0.0), axis=1, keepdims=True)
        for i in range(3)
    )
    return (low + middle) + high


def fill_gates(parts, gate, expert, experts):
    def body(rows):
        column = gate_column(parts[rows, :], expert, experts)
        gate[rows, :] = jnp.broadcast_to(column, (column.shape[0], gate.shape[1]))

    each_rows(parts.shape[0], body)


def held_expert(flags):
    me = lax.axis_index("expert")
    flag = flags[me]
    return me, jnp.where(flag > 0, me ^ (lax.axis_size("expert") // 2), me), flag


def stage_kernel(*refs):
    weight, out, sems = refs[-3:]
    wait(started(sems, 0, [(weight.at[:, c], out.at[:, c]) for c in columns(weight.shape[1])]))


def zero_kernel(*refs):
    refs[-1][...] = jnp.zeros_like(refs[-1])


def hidden_kernel(xa, xb, win, after, act, silu, slope, x, hidden, sems):
    units, rows_all = act.shape
    dim = win.shape[1]
    loads = []
    for c, cols in enumerate(columns(dim)):
        loads.append(started(sems, 2 * c, row_copies(xa, xb, x, cols)))
    for c, cols in enumerate(columns(dim)):
        wait(loads[c])

        def multiply(rows):
            product = nt(win[:, cols], x[rows, cols])
            hidden[:, rows] = product if c == 0 else hidden[:, rows] + product

        each_rows(rows_all, multiply)

    def pointwise(rows):
        g, u = hidden[pl.ds(0, units), rows], hidden[pl.ds(units, units), rows]
        sig = jax.nn.sigmoid(g)
        gated = g * sig
        silu[:, rows] = gated
        slope[:, rows] = u * sig * (1.0 + g * (1.0 - sig))
        act[:, rows] = (gated * u).astype(BF16)

    each_rows(rows_all, pointwise)


def split_product(rows_ref, weight, keep, send, finish):
    half, dim = send.shape
    for cols in columns(dim):

        def multiply(start, target):
            def body(rows):
                mine = pl.ds(rows.start + start, rows.size)
                product = nn(rows_ref[mine, :], weight[:, cols]).astype(BF16)
                target[rows, cols] = finish(mine, product)

            return body

        each_rows(half, multiply(half, send))
        each_rows(half, multiply(0, keep))


def part_kernel(
    experts, flags, xa, xb, act, wdown, keep, send, gate, gate_held, parts, rows_act, sems
):
    dim = wdown.shape[1]
    rows_all, width = parts.shape
    loads = started(sems, 0, row_copies(xa, xb, parts, pl.ds(dim, width), pl.ds(0, width)))

    def turn(rows):
        rows_act[rows, :] = act[:, rows].T

    each_rows(rows_all, turn)
    me, held, _ = held_expert(flags)
    wait(loads)
    fill_gates(parts, gate, me, experts)
    fill_gates(parts, gate_held, held, experts)

    def weighted(rows, part):
        return (gate[rows, pl.ds(0, 1)] * part.astype(F32)).astype(BF16)

    split_product(rows_act, wdown, keep, send, weighted)


def back_kernel(factors, win, after, keep, send, rows_grad):
    units = win.shape[0] // 2

    def turn(rows):
        rows_grad[rows, :] = factors[pl.ds(units, 2 * units), rows].T

    each_rows(rows_grad.shape[0], turn)
    split_product(rows_grad, win, keep, send, lambda rows, part: part)


def factor_kernel(
    ya, yb, act, silu, slope, gate, wdown, after, factors, y, total, sems
):
    units, dim = wdown.shape
    rows_all = y.shape[0]
    loads = []
    for c, cols in enumerate(columns(dim)):
        loads.append(started(sems, 2 * c, row_copies(ya, yb, y, cols)))
    factors[pl.ds(0, units), :] = act[...]
    for c, cols in enumerate(columns(dim)):
        wait(loads[c])

        def multiply(rows):
            scaled = (gate[rows, pl.ds(0, 1)] * y[rows, cols].astype(F32)).astype(BF16)
            product = nt(wdown[:, cols], scaled)
            total[:, rows] = product if c == 0 else total[:, rows] + product

        each_rows(rows_all, multiply)

    def pointwise(rows):
        value = total[:, rows]
        factors[pl.ds(units, units), rows] = (value * slope[:, rows]).astype(BF16)
        factors[pl.ds(2 * units, units), rows] = (value * silu[:, rows]).astype(BF16)

    each_rows(rows_all, pointwise)


def weight_kernel(first, scaled, flags, own, away, gate, ra, rb, *rest):
    grads, r, used, out, sems = rest[-5:]
    groups, units, dim = grads.shape
    rows_all = r.shape[0]
    base, loads, stores = 0, [], []
    for cols in columns(dim):
        loads.append(started(sems, base, row_copies(ra, rb, r, cols)))
        base += 2
    _, _, flag = held_expert(flags)
    some = pl.ds(first * units, groups * units)
    used[...] = jnp.where(flag > 0, away[some, :], own[some, :])
    for c, cols in enumerate(columns(dim)):
        wait(loads[c])
        if scaled:

            def scale(rows):
                r[rows, cols] = (gate[rows, pl.ds(0, 1)] * r[rows, cols].astype(F32)).astype(BF16)

            each_rows(rows_all, scale)
        pairs = []
        for i in range(groups):
            some = pl.ds(i * units, units)
            out[some, cols] = nn(used[some, :], r[:, cols]).astype(BF16)
            pairs.append((out.at[some, cols], grads.at[i, :, cols]))
        stores.append(started(sems, base, pairs))
        base += groups
    for store in stores:
        wait(store)


def rounded_up(value, unit):
    return -(-value // unit) * unit


def params(mib):
    return pltpu.CompilerParams(vmem_limit_bytes=mib * 1024 * 1024)


def cost(flops, size):
    return pl.CostEstimate(flops=flops, bytes_accessed=size, transcendentals=0)


def masks(axis):
    size, out = lax.axis_size(axis), []
    while size > 1:
        size //= 2
        out.append((axis, size))
    return out


def partner(block, bit):
    axis, mask = bit
    return lax.ppermute(block, axis, [(i, i ^ mask) for i in range(lax.axis_size(axis))])


def inner_rows(bit, done, order, unit):
    for other in done:
        if order.index(other) > order.index(bit):
            unit *= 2
    return unit


def join(a, b, inner):
    pair = [part.reshape(-1, inner, part.shape[-1]) for part in (a, b)]
    return jnp.concatenate(pair, axis=1).reshape(-1, a.shape[-1])


def halves(block, inner):
    split = block.reshape(-1, 2, inner, block.shape[1])
    return [split[:, i].reshape(-1, block.shape[1]) for i in (0, 1)]


def is_set(bit):
    return (lax.axis_index(bit[0]) & bit[1]) > 0


def add(a, b):
    return (a.astype(F32) + b.astype(F32)).astype(BF16)


def on_device(tokens, cotangent, gates, expert_ids, swap_flag, w_in, w_down):
    experts = lax.axis_size("expert")
    half_axis = experts // 2
    tok_dev, dim = tokens.shape
    units = w_down.shape[1]

    across, within = masks("dp"), masks("expert")
    core, near, far = within[-1], within[-2:-1], within[:-2]
    first = near + across
    second = across + near
    order = first[::-1] + far[::-1]
    rows_all = tok_dev * lax.axis_size("dp") * experts
    top = far[0]

    slots = jnp.arange(experts, dtype=jnp.int32)
    dense = jnp.sum(
        jnp.where(expert_ids[:, :, None] == slots, gates[:, :, None], 0.0), axis=1
    )
    parts = jnp.concatenate(split_three(dense), axis=1)
    width = rounded_up(parts.shape[1], 128)
    parts = jnp.pad(parts, ((0, 0), (0, width - parts.shape[1])))
    payload = jnp.stack([jnp.concatenate([rows, parts], axis=1) for rows in (tokens, cotangent)])

    def far_gather(block):
        for i in range(0, len(far), 2):
            group = far[i : i + 2]

            def arrived(rows, bit):
                return partner(rows.reshape(-1, rows.shape[2]), bit).reshape(rows.shape)

            a = group[0]
            across = arrived(block, a)
            if len(group) == 2:
                b = group[1]
                pairs = [jnp.concatenate([rows, arrived(rows, b)], axis=1) for rows in (block, across)]
            else:
                pairs = [block, across]
            if a == top:
                turn = is_set(top)
                pairs = [jnp.where(turn, pairs[1 - j], pairs[j]) for j in (0, 1)]
            block = jnp.concatenate(pairs, axis=1)
        return block

    def plane_step_out(rows, route, k, zero=None):
        got = partner(rows, route[k])
        got = got if zero is None else got + zero
        return join(rows, got, inner_rows(route[k], route[:k], order, far_rows))

    def zero_after(columns_of, *arrays):
        return pl.pallas_call(
            zero_kernel,
            out_shape=jax.ShapeDtypeStruct((16, columns_of), BF16),
            in_specs=[ANY] * len(arrays),
            out_specs=VMEM,
            compiler_params=params(2),
            name="zero",
        )(*arrays)[:1]

    def stage(weight, after, name):
        return pl.pallas_call(
            stage_kernel,
            out_shape=jax.ShapeDtypeStruct(weight.shape, BF16),
            in_specs=[ANY] * (len(after) + 1),
            out_specs=VMEM,
            scratch_shapes=[pltpu.SemaphoreType.DMA((CHUNKS,))],
            compiler_params=params(STAGE_MIB),
            cost_estimate=cost(0, 4 * weight.size),
            name=name,
        )(*after, weight)

    x_far, y_far = far_gather(payload)
    far_rows = x_far.shape[0]
    xa, ya = x_far, y_far
    for k in range(len(first)):
        zero = None
        if k == len(first) - 1:
            win = stage(w_in.reshape(2 * units, dim), (xa, ya), "stage_in")
            wdown = stage(w_down.reshape(units, dim), (xa, ya), "stage_down")
            zero = zero_after(dim + width, win, wdown)
        xa, ya = plane_step_out(xa, first, k, zero), plane_step_out(ya, second, k)
    xb, yb = partner(xa, core), partner(ya, core)

    half_rows = rows_all // 2
    limit = 60 if rows_all > 512 else 24
    row_type = jax.ShapeDtypeStruct((half_rows, dim), BF16)
    gate_type = jax.ShapeDtypeStruct((rows_all, 128), F32)
    saved_type = jax.ShapeDtypeStruct((units, rows_all), F32)
    product = 2 * rows_all * units * dim
    act, silu, slope = pl.pallas_call(
        hidden_kernel,
        out_shape=[
            jax.ShapeDtypeStruct((units, rows_all), BF16),
            saved_type,
            saved_type,
        ],
        in_specs=[ANY, ANY, VMEM, ANY],
        out_specs=[VMEM] * 3,
        scratch_shapes=[
            pltpu.VMEM((rows_all, dim), BF16),
            pltpu.VMEM((2 * units, rows_all), F32),
            pltpu.SemaphoreType.DMA((2 * CHUNKS,)),
        ],
        compiler_params=params(limit),
        cost_estimate=cost(2 * product, 4 * dim * (units + rows_all)),
        name="hidden",
    )(xa, xb, win, wdown)
    mixed_keep, mixed_send, gate, gate_held = pl.pallas_call(
        functools.partial(part_kernel, experts),
        out_shape=[row_type, row_type, gate_type, gate_type],
        in_specs=[SMEM, ANY, ANY, VMEM, VMEM],
        out_specs=[VMEM] * 4,
        scratch_shapes=[
            pltpu.VMEM((rows_all, width), BF16),
            pltpu.VMEM((rows_all, units), BF16),
            pltpu.SemaphoreType.DMA((2,)),
        ],
        compiler_params=params(limit),
        cost_estimate=cost(product, 2 * dim * (units + rows_all)),
        name="part",
    )(swap_flag, xa, xb, act, wdown)
    factors = pl.pallas_call(
        factor_kernel,
        out_shape=jax.ShapeDtypeStruct((3 * units, rows_all), BF16),
        in_specs=[ANY] * 2 + [VMEM] * 5 + [ANY],
        out_specs=VMEM,
        scratch_shapes=[
            pltpu.VMEM((rows_all, dim), BF16),
            pltpu.VMEM((units, rows_all), F32),
            pltpu.SemaphoreType.DMA((2 * CHUNKS,)),
        ],
        compiler_params=params(limit),
        cost_estimate=cost(product, 2 * dim * (units + rows_all)),
        name="factors",
    )(ya, yb, act, silu, slope, gate, wdown, mixed_send)
    far_factors = partner(factors, ("expert", half_axis))
    mixed_got = partner(mixed_send, core)
    back_keep, back_send = pl.pallas_call(
        back_kernel,
        out_shape=[row_type, row_type],
        in_specs=[VMEM] * 2 + [ANY],
        out_specs=[VMEM] * 2,
        scratch_shapes=[pltpu.VMEM((rows_all, 2 * units), BF16)],
        compiler_params=params(limit),
        cost_estimate=cost(2 * product, 4 * dim * (units + rows_all)),
        name="back",
    )(factors, win, mixed_got)

    def added(keep, got, bit, left):
        inner = inner_rows(bit, left, order, tok_dev)
        return [add(*pair) for pair in zip(halves(keep, inner), halves(got, inner))]

    def far_sum(rows, group, late=None):
        a = group[0]
        inner = rows.shape[0] // 2
        pair = [rows[:inner], rows[inner:]]
        if a == top:
            turn = is_set(top)
            pair = [jnp.where(turn, pair[1 - j], pair[j]) for j in (0, 1)]
        if len(group) == 1:
            onward = pair[1] if late is None else pair[1] + late(pair[1])
            return add(pair[0], partner(onward, a)), onward
        b = group[1]
        low = inner // 2
        furthest, beside = pair[1][low:], pair[0][low:]
        onward = add(pair[1][:low], partner(furthest, b))
        if late is not None:
            onward = onward + late(furthest, beside)
        total = pair[0][:low].astype(F32) + partner(beside, b).astype(F32)
        return (total + partner(onward, a).astype(F32)).astype(BF16), onward

    groups = [far[i : i + 2] for i in range(0, len(far), 2)]

    def plane_step(keep, got, route, k):
        left = set(order) - set(route[: k + 1])
        keep, sent = added(keep, got, route[k], left)
        return keep, partner(sent, route[k]), sent

    def weight_gradient(after, first, groups, pieces, scaled, name):
        return pl.pallas_call(
            functools.partial(weight_kernel, first, scaled),
            out_shape=jax.ShapeDtypeStruct((groups, units, dim), BF16),
            in_specs=[SMEM] + [VMEM] * 3 + [ANY] * (2 + len(after)),
            out_specs=ANY,
            scratch_shapes=[
                pltpu.VMEM((rows_all, dim), BF16),
                pltpu.VMEM((groups * units, rows_all), BF16),
                pltpu.VMEM((groups * units, dim), BF16),
                pltpu.SemaphoreType.DMA(((2 + groups) * CHUNKS,)),
            ],
            compiler_params=params(limit),
            cost_estimate=cost(groups * product, 2 * dim * (groups * units + rows_all)),
            name=name,
        )(swap_flag, factors, far_factors, gate_held, *pieces, *after)

    across_first, near_first = first[::-1], second[::-1]
    back_got = partner(back_send, core)
    for k in range(len(first)):
        if k > 0:
            mixed_got = mixed_got + zero_after(dim, back_sent)
        mixed_keep, mixed_got, mixed_sent = plane_step(mixed_keep, mixed_got, across_first, k)
        back_keep, back_got, back_sent = plane_step(back_keep, back_got, near_first, k)
    both = jnp.concatenate([add(mixed_keep, mixed_got), add(back_keep, back_got)], axis=1)
    for group in groups[:0:-1]:
        both, _ = far_sum(both, group)
    both, sent = far_sum(both, groups[0], lambda *ahead: zero_after(2 * dim, far_factors, *ahead))
    mixed, grad_tokens = both[:, :dim], both[:, dim:]
    behind = [sent]
    new_down = weight_gradient(behind, 0, 1, (ya, yb), True, "grad_down")
    new_in = weight_gradient(behind, 1, 2, (xa, xb), False, "grad_in")
    return (mixed, grad_tokens, new_in.reshape(w_in.shape), new_down.reshape(w_down.shape))


def solution(mesh):
    rows = P(("dp", "expert"), None)
    w_in, w_down = P("expert", None, "dp", None), P("expert", "dp", None)
    return jax.shard_map(
        on_device,
        mesh=mesh,
        in_specs=(rows, rows, rows, rows, P(), w_in, w_down),
        out_specs=(rows, rows, w_in, w_down),
        check_vma=False,
    )
```

```python
import functools

import jax
import jax.numpy as jnp
from jax import lax
from jax.experimental import pallas as pl
from jax.experimental.pallas import tpu as pltpu
from jax.sharding import PartitionSpec as P

F32, BF16 = jnp.float32, jnp.bfloat16
ANY = pl.BlockSpec(memory_space=pl.ANY)
SMEM = pl.BlockSpec(memory_space=pltpu.SMEM)
VMEM = pl.BlockSpec(memory_space=pltpu.VMEM)
CHUNKS = 4
ROW_BLOCK = 256
STAGE_MIB = 40


def nt(a, b):
    return lax.dot_general(a, b, (((1,), (1,)), ((), ())), preferred_element_type=F32)


def nn(a, b):
    return jnp.dot(a, b, preferred_element_type=F32)


def each_rows(total, body):
    if total <= ROW_BLOCK:
        body(pl.ds(0, total))
    else:

        @pl.loop(0, total // ROW_BLOCK)
        def _(i):
            body(pl.ds(pl.multiple_of(i * ROW_BLOCK, ROW_BLOCK), ROW_BLOCK))


def columns(dim):
    step = dim // CHUNKS
    return [pl.ds(c * step, step) for c in range(CHUNKS)]


def started(sems, base, pairs):
    copies = [
        pltpu.make_async_copy(source, target, sems.at[base + i])
        for i, (source, target) in enumerate(pairs)
    ]
    for copy in copies:
        copy.start()
    return copies


def wait(copies):
    for copy in copies:
        copy.wait()


def row_copies(own, received, buffer, cols, target=None):
    half = own.shape[0]
    target = cols if target is None else target
    return [
        (own.at[:, cols], buffer.at[pl.ds(0, half), target]),
        (received.at[:, cols], buffer.at[pl.ds(half, half), target]),
    ]


def split_three(x):
    high = x.astype(BF16)
    rest = x - high.astype(F32)
    middle = rest.astype(BF16)
    low = (rest - middle.astype(F32)).astype(BF16)
    return high, middle, low


def gate_column(parts, expert, experts):
    lane = lax.broadcasted_iota(jnp.int32, parts.shape, 1)
    values = parts.astype(F32)
    high, middle, low = (
        jnp.sum(jnp.where(lane == expert + i * experts, values, 0.0), axis=1, keepdims=True)
        for i in range(3)
    )
    return (low + middle) + high


def fill_gates(parts, gate, expert, experts):
    def body(rows):
        column = gate_column(parts[rows, :], expert, experts)
        gate[rows, :] = jnp.broadcast_to(column, (column.shape[0], gate.shape[1]))

    each_rows(parts.shape[0], body)


def held_expert(flags):
    me = lax.axis_index("expert")
    flag = flags[me]
    return me, jnp.where(flag > 0, me ^ (lax.axis_size("expert") // 2), me), flag


def stage_kernel(*refs):
    weight, out, sems = refs[-3:]
    wait(started(sems, 0, [(weight.at[:, c], out.at[:, c]) for c in columns(weight.shape[1])]))


def zero_kernel(*refs):
    refs[-1][...] = jnp.zeros_like(refs[-1])


def hidden_kernel(xa, xb, win, after, act, silu, slope, x, hidden, sems):
    units, rows_all = act.shape
    dim = win.shape[1]
    loads = []
    for c, cols in enumerate(columns(dim)):
        loads.append(started(sems, 2 * c, row_copies(xa, xb, x, cols)))
    for c, cols in enumerate(columns(dim)):
        wait(loads[c])

        def multiply(rows):
            product = nt(win[:, cols], x[rows, cols])
            hidden[:, rows] = product if c == 0 else hidden[:, rows] + product

        each_rows(rows_all, multiply)

    def pointwise(rows):
        g, u = hidden[pl.ds(0, units), rows], hidden[pl.ds(units, units), rows]
        sig = jax.nn.sigmoid(g)
        gated = g * sig
        silu[:, rows] = gated
        slope[:, rows] = u * sig * (1.0 + g * (1.0 - sig))
        act[:, rows] = (gated * u).astype(BF16)

    each_rows(rows_all, pointwise)


def split_product(rows_ref, weight, keep, send, finish):
    half, dim = send.shape
    for cols in columns(dim):

        def multiply(start, target):
            def body(rows):
                mine = pl.ds(rows.start + start, rows.size)
                product = nn(rows_ref[mine, :], weight[:, cols]).astype(BF16)
                target[rows, cols] = finish(mine, product)

            return body

        each_rows(half, multiply(half, send))
        each_rows(half, multiply(0, keep))


def part_kernel(
    experts, flags, xa, xb, act, wdown, keep, send, gate, gate_held, parts, rows_act, sems
):
    dim = wdown.shape[1]
    rows_all, width = parts.shape
    loads = started(sems, 0, row_copies(xa, xb, parts, pl.ds(dim, width), pl.ds(0, width)))

    def turn(rows):
        rows_act[rows, :] = act[:, rows].T

    each_rows(rows_all, turn)
    me, held, _ = held_expert(flags)
    wait(loads)
    fill_gates(parts, gate, me, experts)
    fill_gates(parts, gate_held, held, experts)

    def weighted(rows, part):
        return (gate[rows, pl.ds(0, 1)] * part.astype(F32)).astype(BF16)

    split_product(rows_act, wdown, keep, send, weighted)


def back_kernel(factors, win, after, keep, send, rows_grad):
    units = win.shape[0] // 2

    def turn(rows):
        rows_grad[rows, :] = factors[pl.ds(units, 2 * units), rows].T

    each_rows(rows_grad.shape[0], turn)
    split_product(rows_grad, win, keep, send, lambda rows, part: part)


def factor_kernel(
    ya, yb, act, silu, slope, gate, wdown, after, factors, y, total, sems
):
    units, dim = wdown.shape
    rows_all = y.shape[0]
    loads = []
    for c, cols in enumerate(columns(dim)):
        loads.append(started(sems, 2 * c, row_copies(ya, yb, y, cols)))
    factors[pl.ds(0, units), :] = act[...]
    for c, cols in enumerate(columns(dim)):
        wait(loads[c])

        def multiply(rows):
            scaled = (gate[rows, pl.ds(0, 1)] * y[rows, cols].astype(F32)).astype(BF16)
            product = nt(wdown[:, cols], scaled)
            total[:, rows] = product if c == 0 else total[:, rows] + product

        each_rows(rows_all, multiply)

    def pointwise(rows):
        value = total[:, rows]
        factors[pl.ds(units, units), rows] = (value * slope[:, rows]).astype(BF16)
        factors[pl.ds(2 * units, units), rows] = (value * silu[:, rows]).astype(BF16)

    each_rows(rows_all, pointwise)


def weight_kernel(first, scaled, flags, own, away, gate, ra, rb, *rest):
    grads, r, used, out, sems = rest[-5:]
    groups, units, dim = grads.shape
    rows_all = r.shape[0]
    base, loads, stores = 0, [], []
    for cols in columns(dim):
        loads.append(started(sems, base, row_copies(ra, rb, r, cols)))
        base += 2
    _, _, flag = held_expert(flags)
    some = pl.ds(first * units, groups * units)
    used[...] = jnp.where(flag > 0, away[some, :], own[some, :])
    for c, cols in enumerate(columns(dim)):
        wait(loads[c])
        if scaled:

            def scale(rows):
                r[rows, cols] = (gate[rows, pl.ds(0, 1)] * r[rows, cols].astype(F32)).astype(BF16)

            each_rows(rows_all, scale)
        pairs = []
        for i in range(groups):
            some = pl.ds(i * units, units)
            out[some, cols] = nn(used[some, :], r[:, cols]).astype(BF16)
            pairs.append((out.at[some, cols], grads.at[i, :, cols]))
        stores.append(started(sems, base, pairs))
        base += groups
    for store in stores:
        wait(store)


def rounded_up(value, unit):
    return -(-value // unit) * unit


def params(mib):
    return pltpu.CompilerParams(vmem_limit_bytes=mib * 1024 * 1024)


def cost(flops, size):
    return pl.CostEstimate(flops=flops, bytes_accessed=size, transcendentals=0)


def masks(axis):
    size, out = lax.axis_size(axis), []
    while size > 1:
        size //= 2
        out.append((axis, size))
    return out


def partner(block, bit):
    axis, mask = bit
    return lax.ppermute(block, axis, [(i, i ^ mask) for i in range(lax.axis_size(axis))])


def inner_rows(bit, done, order, unit):
    for other in done:
        if order.index(other) > order.index(bit):
            unit *= 2
    return unit


def join(a, b, inner):
    pair = [part.reshape(-1, inner, part.shape[-1]) for part in (a, b)]
    return jnp.concatenate(pair, axis=1).reshape(-1, a.shape[-1])


def halves(block, inner):
    split = block.reshape(-1, 2, inner, block.shape[1])
    return [split[:, i].reshape(-1, block.shape[1]) for i in (0, 1)]


def is_set(bit):
    return (lax.axis_index(bit[0]) & bit[1]) > 0


def add(a, b):
    return (a.astype(F32) + b.astype(F32)).astype(BF16)


def on_device(tokens, cotangent, gates, expert_ids, swap_flag, w_in, w_down):
    experts = lax.axis_size("expert")
    half_axis = experts // 2
    tok_dev, dim = tokens.shape
    units = w_down.shape[1]

    across, within = masks("dp"), masks("expert")
    core, near, far = within[-1], within[-2:-1], within[:-2]
    first = near + across
    second = across + near
    order = first[::-1] + far[::-1]
    rows_all = tok_dev * lax.axis_size("dp") * experts
    top = far[0]

    slots = jnp.arange(experts, dtype=jnp.int32)
    dense = jnp.sum(
        jnp.where(expert_ids[:, :, None] == slots, gates[:, :, None], 0.0), axis=1
    )
    parts = jnp.concatenate(split_three(dense), axis=1)
    width = rounded_up(parts.shape[1], 128)
    parts = jnp.pad(parts, ((0, 0), (0, width - parts.shape[1])))
    payload = jnp.stack([jnp.concatenate([rows, parts], axis=1) for rows in (tokens, cotangent)])

    def far_gather(block):
        for i in range(0, len(far), 2):
            group = far[i : i + 2]

            def arrived(rows, bit):
                return partner(rows.reshape(-1, rows.shape[2]), bit).reshape(rows.shape)

            a = group[0]
            across = arrived(block, a)
            if len(group) == 2:
                b = group[1]
                pairs = [jnp.concatenate([rows, arrived(rows, b)], axis=1) for rows in (block, across)]
            else:
                pairs = [block, across]
            if a == top:
                turn = is_set(top)
                pairs = [jnp.where(turn, pairs[1 - j], pairs[j]) for j in (0, 1)]
            block = jnp.concatenate(pairs, axis=1)
        return block

    def plane_step_out(rows, route, k, zero=None):
        got = partner(rows, route[k])
        got = got if zero is None else got + zero
        return join(rows, got, inner_rows(route[k], route[:k], order, far_rows))

    def zero_after(columns_of, *arrays):
        return pl.pallas_call(
            zero_kernel,
            out_shape=jax.ShapeDtypeStruct((16, columns_of), BF16),
            in_specs=[ANY] * len(arrays),
            out_specs=VMEM,
            compiler_params=params(2),
            name="zero",
        )(*arrays)[:1]

    def stage(weight, after, name):
        return pl.pallas_call(
            stage_kernel,
            out_shape=jax.ShapeDtypeStruct(weight.shape, BF16),
            in_specs=[ANY] * (len(after) + 1),
            out_specs=VMEM,
            scratch_shapes=[pltpu.SemaphoreType.DMA((CHUNKS,))],
            compiler_params=params(STAGE_MIB),
            cost_estimate=cost(0, 4 * weight.size),
            name=name,
        )(*after, weight)

    x_far, y_far = far_gather(payload)
    far_rows = x_far.shape[0]
    xa, ya = x_far, y_far
    for k in range(len(first)):
        zero = None
        if k == len(first) - 1:
            win = stage(w_in.reshape(2 * units, dim), (xa, ya), "stage_in")
            wdown = stage(w_down.reshape(units, dim), (xa, ya), "stage_down")
            zero = zero_after(dim + width, win, wdown)
        xa, ya = plane_step_out(xa, first, k, zero), plane_step_out(ya, second, k)
    xb, yb = partner(xa, core), partner(ya, core)

    half_rows = rows_all // 2
    limit = 60 if rows_all > 512 else 24
    row_type = jax.ShapeDtypeStruct((half_rows, dim), BF16)
    gate_type = jax.ShapeDtypeStruct((rows_all, 128), F32)
    saved_type = jax.ShapeDtypeStruct((units, rows_all), F32)
    product = 2 * rows_all * units * dim
    act, silu, slope = pl.pallas_call(
        hidden_kernel,
        out_shape=[
            jax.ShapeDtypeStruct((units, rows_all), BF16),
            saved_type,
            saved_type,
        ],
        in_specs=[ANY, ANY, VMEM, ANY],
        out_specs=[VMEM] * 3,
        scratch_shapes=[
            pltpu.VMEM((rows_all, dim), BF16),
            pltpu.VMEM((2 * units, rows_all), F32),
            pltpu.SemaphoreType.DMA((2 * CHUNKS,)),
        ],
        compiler_params=params(limit),
        cost_estimate=cost(2 * product, 4 * dim * (units + rows_all)),
        name="hidden",
    )(xa, xb, win, wdown)
    mixed_keep, mixed_send, gate, gate_held = pl.pallas_call(
        functools.partial(part_kernel, experts),
        out_shape=[row_type, row_type, gate_type, gate_type],
        in_specs=[SMEM, ANY, ANY, VMEM, VMEM],
        out_specs=[VMEM] * 4,
        scratch_shapes=[
            pltpu.VMEM((rows_all, width), BF16),
            pltpu.VMEM((rows_all, units), BF16),
            pltpu.SemaphoreType.DMA((2,)),
        ],
        compiler_params=params(limit),
        cost_estimate=cost(product, 2 * dim * (units + rows_all)),
        name="part",
    )(swap_flag, xa, xb, act, wdown)
    factors = pl.pallas_call(
        factor_kernel,
        out_shape=jax.ShapeDtypeStruct((3 * units, rows_all), BF16),
        in_specs=[ANY] * 2 + [VMEM] * 5 + [ANY],
        out_specs=VMEM,
        scratch_shapes=[
            pltpu.VMEM((rows_all, dim), BF16),
            pltpu.VMEM((units, rows_all), F32),
            pltpu.SemaphoreType.DMA((2 * CHUNKS,)),
        ],
        compiler_params=params(limit),
        cost_estimate=cost(product, 2 * dim * (units + rows_all)),
        name="factors",
    )(ya, yb, act, silu, slope, gate, wdown, mixed_send)
    mixed_got = partner(mixed_send, core)
    back_keep, back_send = pl.pallas_call(
        back_kernel,
        out_shape=[row_type, row_type],
        in_specs=[VMEM] * 2 + [ANY],
        out_specs=[VMEM] * 2,
        scratch_shapes=[pltpu.VMEM((rows_all, 2 * units), BF16)],
        compiler_params=params(limit),
        cost_estimate=cost(2 * product, 4 * dim * (units + rows_all)),
        name="back",
    )(factors, win, mixed_got)

    def added(keep, got, bit, left):
        inner = inner_rows(bit, left, order, tok_dev)
        return [add(*pair) for pair in zip(halves(keep, inner), halves(got, inner))]

    def far_sum(rows, group, late=None):
        a = group[0]
        inner = rows.shape[0] // 2
        pair = [rows[:inner], rows[inner:]]
        if a == top:
            turn = is_set(top)
            pair = [jnp.where(turn, pair[1 - j], pair[j]) for j in (0, 1)]
        if len(group) == 1:
            onward = pair[1] if late is None else pair[1] + late(pair[1])
            return add(pair[0], partner(onward, a)), onward
        b = group[1]
        low = inner // 2
        furthest, beside = pair[1][low:], pair[0][low:]
        onward = add(pair[1][:low], partner(furthest, b))
        if late is not None:
            onward = onward + late(furthest, beside)
        total = pair[0][:low].astype(F32) + partner(beside, b).astype(F32)
        return (total + partner(onward, a).astype(F32)).astype(BF16), onward

    groups = [far[i : i + 2] for i in range(0, len(far), 2)]

    def plane_step(keep, got, route, k):
        left = set(order) - set(route[: k + 1])
        keep, sent = added(keep, got, route[k], left)
        return keep, partner(sent, route[k]), sent

    def weight_gradient(after, first, groups, pieces, scaled, name):
        return pl.pallas_call(
            functools.partial(weight_kernel, first, scaled),
            out_shape=jax.ShapeDtypeStruct((groups, units, dim), BF16),
            in_specs=[SMEM] + [VMEM] * 3 + [ANY] * (2 + len(after)),
            out_specs=ANY,
            scratch_shapes=[
                pltpu.VMEM((rows_all, dim), BF16),
                pltpu.VMEM((groups * units, rows_all), BF16),
                pltpu.VMEM((groups * units, dim), BF16),
                pltpu.SemaphoreType.DMA(((2 + groups) * CHUNKS,)),
            ],
            compiler_params=params(limit),
            cost_estimate=cost(groups * product, 2 * dim * (groups * units + rows_all)),
            name=name,
        )(swap_flag, factors, far_factors, gate_held, *pieces, *after)

    across_first, near_first = first[::-1], second[::-1]
    back_got = partner(back_send, core)
    for k in range(len(first)):
        if k > 0:
            mixed_got = mixed_got + zero_after(dim, back_sent)
        mixed_keep, mixed_got, mixed_sent = plane_step(mixed_keep, mixed_got, across_first, k)
        if k == 0:
            behind_mixed = factors + zero_after(rows_all, mixed_sent)
            far_factors = partner(behind_mixed, ("expert", half_axis))
        back_keep, back_got, back_sent = plane_step(back_keep, back_got, near_first, k)
    both = jnp.concatenate([add(mixed_keep, mixed_got), add(back_keep, back_got)], axis=1)
    for group in groups[:0:-1]:
        both, _ = far_sum(both, group)
    both, sent = far_sum(both, groups[0], lambda *ahead: zero_after(2 * dim, far_factors, *ahead))
    mixed, grad_tokens = both[:, :dim], both[:, dim:]
    behind = [sent]
    new_down = weight_gradient(behind, 0, 1, (ya, yb), True, "grad_down")
    new_in = weight_gradient(behind, 1, 2, (xa, xb), False, "grad_in")
    return (mixed, grad_tokens, new_in.reshape(w_in.shape), new_down.reshape(w_down.shape))


def solution(mesh):
    rows = P(("dp", "expert"), None)
    w_in, w_down = P("expert", None, "dp", None), P("expert", "dp", None)
    return jax.shard_map(
        on_device,
        mesh=mesh,
        in_specs=(rows, rows, rows, rows, P(), w_in, w_down),
        out_specs=(rows, rows, w_in, w_down),
        check_vma=False,
    )
```
